256 devices in a mesh: cohort: 32 (over x, y, core), snp: 8 (over z).
Axes of the slice: x: 4, y: 4, z: 8, core: 2. Of those that a mesh axis runs over, the one named last changes fastest.
Arguments:
- rhs_animal: float32 [4, 262144], P(None, 'cohort'), may hold values from -40 to 40
- rhs_snp: float32 [4, 51200], P(None, 'snp'), may hold values from -6 to 6
- record_weight: float32 [262144], P('cohort'), may hold values from 0.5 to 2
- sire_index: int32 [262144], P('cohort'), may hold values from -1 to 253951, as said below
- dam_index: int32 [262144], P('cohort'), may hold values from -1 to 253951, as said below
- cohort_sizes: int32 [32], replicated, may hold values from 2048 to 8192, as said below
- geno_index: int32 [8192], P('cohort'), may hold values from 0 to 262143, as said below
- genotypes: float32 [8192, 51200], P('cohort', 'snp'), may hold values from -0.0625 to 0.0625
- precond_animal: float32 [4, 4, 262144], P(None, None, 'cohort'), may hold values from -0.3 to 3, as said below
- precond_snp: float32 [4, 4, 51200], P(None, None, 'snp'), may hold values from -0.3 to 2, as said below
- genetic_inv: float32 [4, 4], replicated, may hold values from -0.3 to 2, as said below
- residual_inv: float32 [4, 4], replicated, may hold values from -0.3 to 2, as said below
- coupling: float32 [4, 4], replicated, may hold values from -0.3 to 2, as said below
- snp_prior: float32 [4, 4], replicated, may hold values from -0.3 to 2, as said below
Outputs:
- solution_animal: float32 [4, 262144], P(None, 'cohort')
- solution_snp: float32 [4, 51200], P(None, 'snp')
- residual_animal: float32 [4, 262144], P(None, 'cohort')
- residual_snp: float32 [4, 51200], P(None, 'snp')
The draws below stay inside these ranges and needn't reach their ends.
Inputs may be any that keep to these rules, and one draw needn't show every extreme that they name: `cohort_sizes`: some cohort has exactly 8192 live animals. `sire_index`: -1, or a live animal born 1 to 3 cohorts before the animal; animals in empty slots have -1. `dam_index`: -1, or a live animal born 1 to 3 cohorts before the animal; animals in empty slots have -1. `geno_index`: entries c * 256 to (c + 1) * 256 - 1 are distinct live animals of cohort c, in rising order. `precond_animal`: each block is symmetric with a dominant diagonal. `precond_snp`: each block is symmetric with a dominant diagonal. `genetic_inv`: symmetric with a dominant diagonal. `residual_inv`: symmetric with a dominant diagonal. `coupling`: symmetric with a dominant diagonal. `snp_prior`: symmetric with a dominant diagonal.
All inputs are finite; a program needn't handle non-finite values.
Results may differ from the reference program's by a relative error of at most 0.00012.
Values sent between devices are 32-bit elements; how exact they have to be, the bound alone decides.
A program may use at most 128 MiB of HBM per device.

```python
import math
import jax
import jax.numpy as jnp
from jax import lax

TRAITS = 4
SNPS = 51200
SPAN = 3
ITERS = 2
ANIM_DEV = 8192
G_DEV = 256
COHORTS = 32
ANIMALS = 262144
GENOTYPED = 8192


def cohort_table(key):
    first, second = jax.random.split(jax.random.fold_in(key, 101))
    sizes = jax.random.randint(first, (COHORTS,), ANIM_DEV // 4, ANIM_DEV + 1)
    fullest = jax.random.randint(second, (), 0, COHORTS)
    sizes = jnp.where(jnp.arange(COHORTS) == fullest, ANIM_DEV, sizes)
    return sizes.astype(jnp.int32)


def parent_draw(key, sizes, unknown_share):
    lag_key, pick_key, miss_key = jax.random.split(key, 3)
    animal_ids = jnp.arange(ANIMALS, dtype=jnp.int32)
    cohort_of = animal_ids // ANIM_DEV
    slot_of = animal_ids % ANIM_DEV
    lag = jax.random.randint(lag_key, (ANIMALS,), 1, SPAN + 1)
    parent_cohort = cohort_of - lag
    picked = jax.random.randint(pick_key, (ANIMALS,), 0, 1 << 30)
    parent_size = sizes[jnp.clip(parent_cohort, 0, COHORTS - 1)]
    parent_slot = picked % parent_size
    present = jax.random.randint(miss_key, (ANIMALS,), 0, 20) >= unknown_share
    known = (parent_cohort >= 0) & (slot_of < sizes[cohort_of]) & present
    return jnp.where(known, parent_cohort * ANIM_DEV + parent_slot, -1).astype(jnp.int32)


def symmetric_blocks(key, count, upper):
    off_key, diag_key = jax.random.split(key)
    offdiag = jax.random.uniform(off_key, (TRAITS, TRAITS, count), jnp.float32, -0.3, 0.3)
    offdiag = 0.5 * (offdiag + jnp.transpose(offdiag, (1, 0, 2)))
    diagonal = jax.random.uniform(diag_key, (TRAITS, 1, count), jnp.float32, 1.0, upper)
    identity = jnp.eye(TRAITS, dtype=jnp.float32)[:, :, None]
    return offdiag * (1.0 - identity) + identity * diagonal


def draw_cohort_sizes(key, part):
    return cohort_table(key)


def draw_sire_index(key, part):
    sizes = cohort_table(key)
    key = jax.random.fold_in(key, 7)
    return parent_draw(key, sizes, 3)


def draw_dam_index(key, part):
    sizes = cohort_table(key)
    key = jax.random.fold_in(key, 9)
    return parent_draw(key, sizes, 5)


def draw_geno_index(key, part):
    sizes = cohort_table(key)
    key = jax.random.fold_in(key, 11)
    entry = jnp.arange(GENOTYPED, dtype=jnp.int32)
    cohort_of = entry // G_DEV
    within = entry % G_DEV
    size_here = sizes[cohort_of]
    stride = size_here // G_DEV
    offset = jax.random.randint(key, (GENOTYPED,), 0, 1 << 30) % stride
    slot = within * size_here // G_DEV + offset
    return (cohort_of * ANIM_DEV + slot).astype(jnp.int32)


def draw_rhs_animal(key, part):
    key = jax.random.fold_in(key, 3)
    base_key, rough_key = jax.random.split(key, 2)
    animal_ids = jnp.arange(ANIMALS)
    cohort_of = (animal_ids // ANIM_DEV).astype(jnp.float32)
    rise = jnp.exp(math.log(3.0) * cohort_of / (COHORTS - 1))
    rough = jnp.exp(jax.random.uniform(rough_key, (ANIMALS,), jnp.float32, 0.0, math.log(3.0)))
    base = jnp.clip(jax.random.normal(base_key, (TRAITS, ANIMALS), jnp.float32), -4.0, 4.0)
    return base * rise[None, :] * rough[None, :]


def draw_precond_animal(key, part):
    key = jax.random.fold_in(key, 13)
    return symmetric_blocks(key, ANIMALS, 2.0)


def draw_precond_snp(key, part):
    key = jax.random.fold_in(key, 17)
    return symmetric_blocks(key, SNPS, 2.0)


def draw_genetic_inv(key, part):
    key = jax.random.fold_in(key, 19)
    return symmetric_blocks(key, 1, 2.0)[:, :, 0]


def draw_residual_inv(key, part):
    key = jax.random.fold_in(key, 23)
    return symmetric_blocks(key, 1, 2.0)[:, :, 0]


def draw_coupling(key, part):
    key = jax.random.fold_in(key, 29)
    return symmetric_blocks(key, 1, 2.0)[:, :, 0]


def draw_snp_prior(key, part):
    key = jax.random.fold_in(key, 31)
    return symmetric_blocks(key, 1, 2.0)[:, :, 0]


def block_levels(own_key, dims, cuts, smallest, top_value):
    level = 1.0
    for position, blocks in cuts:
        heights = jax.random.uniform(jax.random.fold_in(jax.random.fold_in(own_key, 6), position), (blocks,), jnp.float32, smallest / len(cuts), top_value / len(cuts))
        level = level * jnp.repeat(jnp.exp(heights), dims[position] // blocks).reshape((-1,) + (1,) * (len(dims) - 1 - position))
    return level


def noise(stream_key, shape, scale, bound, cuts=(), held_as=jnp.bfloat16):
    level = block_levels(stream_key, shape, cuts, -0.22, 0.18) if cuts else 1.0
    entries = jax.random.normal(stream_key, shape, jnp.float32) * scale * level
    return jnp.minimum(jnp.maximum(entries, -bound), bound).astype(held_as)


def setup_inputs(seed: int = 0) -> dict:
    arg_keys = jax.random.split(jax.random.key(seed), 15)
    return {
        "rhs_animal": draw_rhs_animal(jax.random.fold_in(arg_keys[14], 71), 0),
        "rhs_snp": noise(arg_keys[1], (TRAITS, SNPS), 1.0, 6.0, ((1, 8),), jnp.float32),
        "record_weight": jnp.clip(jnp.exp(math.log(2.0) - 1.3862944 * jax.random.uniform(arg_keys[2], (ANIMALS,), jnp.float32) ** block_levels(arg_keys[2], (ANIMALS,), ((0, 32),), -0.2, 0.2)), 0.5, 2.0),
        "sire_index": draw_sire_index(jax.random.fold_in(arg_keys[14], 71), 0),
        "dam_index": draw_dam_index(jax.random.fold_in(arg_keys[14], 71), 0),
        "cohort_sizes": draw_cohort_sizes(jax.random.fold_in(arg_keys[14], 71), 0),
        "geno_index": draw_geno_index(jax.random.fold_in(arg_keys[14], 71), 0),
        "genotypes": noise(arg_keys[7], (GENOTYPED, SNPS), GENOTYPED ** -0.5, 0.0625, ((0, 32), (1, 8)), jnp.float32),
        "precond_animal": draw_precond_animal(jax.random.fold_in(arg_keys[14], 71), 0),
        "precond_snp": draw_precond_snp(jax.random.fold_in(arg_keys[14], 71), 0),
        "genetic_inv": draw_genetic_inv(jax.random.fold_in(arg_keys[14], 71), 0),
        "residual_inv": draw_residual_inv(jax.random.fold_in(arg_keys[14], 71), 0),
        "coupling": draw_coupling(jax.random.fold_in(arg_keys[14], 71), 0),
        "snp_prior": draw_snp_prior(jax.random.fold_in(arg_keys[14], 71), 0),
    }


def matmul(left, right):
    return jnp.dot(left, right, precision=lax.Precision.HIGHEST)


def pedigree_inverse(field, sire_index, dam_index):
    count = field.shape[1]
    padded = jnp.concatenate([field, jnp.zeros((field.shape[0], 1), jnp.float32)], axis=1)
    sire_pos = jnp.where(sire_index >= 0, sire_index, count).astype(jnp.int32)
    dam_pos = jnp.where(dam_index >= 0, dam_index, count).astype(jnp.int32)
    known = (sire_index >= 0).astype(jnp.float32) + (dam_index >= 0).astype(jnp.float32)
    factor = 4.0 / (4.0 - known)
    mendel = factor * (field - 0.5 * padded[:, sire_pos] - 0.5 * padded[:, dam_pos])
    back = jnp.zeros((field.shape[0], count + 1), jnp.float32)
    back = back.at[:, sire_pos].add(-0.5 * mendel).at[:, dam_pos].add(-0.5 * mendel)
    return mendel + back[:, :count]


def precondition(blocks, field):
    return jnp.sum(blocks * field[None, :, :], axis=1)


def reference(rhs_animal, rhs_snp, record_weight, sire_index, dam_index, cohort_sizes, geno_index, genotypes, precond_animal, precond_snp, genetic_inv, residual_inv, coupling, snp_prior):
    animal_ids = jnp.arange(ANIMALS, dtype=jnp.int32)
    cohort_of = (animal_ids // ANIM_DEV).astype(jnp.int32)
    slot_of = animal_ids % ANIM_DEV
    live = (slot_of < cohort_sizes[cohort_of]).astype(jnp.float32)
    geno_pos = geno_index.astype(jnp.int32)

    def operate(animal_dir, snp_dir):
        mismatch = animal_dir[:, geno_pos] - matmul(snp_dir, genotypes.T)
        tied = matmul(coupling, mismatch)
        pedigree = pedigree_inverse(animal_dir, sire_index, dam_index)
        out_animal = record_weight[None, :] * matmul(residual_inv, animal_dir) + matmul(genetic_inv, pedigree)
        out_animal = out_animal.at[:, geno_pos].add(tied)
        out_snp = matmul(snp_prior, snp_dir) - matmul(tied, genotypes)
        return out_animal, out_snp

    def inner(left_a, left_s, right_a, right_s):
        return jnp.sum(left_a * right_a) + jnp.sum(left_s * right_s)

    res_animal = rhs_animal * live[None, :]
    res_snp = rhs_snp
    sol_animal = jnp.zeros_like(res_animal)
    sol_snp = jnp.zeros_like(res_snp)
    pre_animal = precondition(precond_animal, res_animal)
    pre_snp = precondition(precond_snp, res_snp)
    dir_animal, dir_snp = pre_animal, pre_snp
    gamma = inner(res_animal, res_snp, pre_animal, pre_snp)
    for step in range(ITERS):
        img_animal, img_snp = operate(dir_animal, dir_snp)
        alpha = gamma / inner(dir_animal, dir_snp, img_animal, img_snp)
        sol_animal = sol_animal + alpha * dir_animal
        sol_snp = sol_snp + alpha * dir_snp
        res_animal = res_animal - alpha * img_animal
        res_snp = res_snp - alpha * img_snp
        if step + 1 < ITERS:
            pre_animal = precondition(precond_animal, res_animal)
            pre_snp = precondition(precond_snp, res_snp)
            gamma_new = inner(res_animal, res_snp, pre_animal, pre_snp)
            dir_animal = pre_animal + (gamma_new / gamma) * dir_animal
            dir_snp = pre_snp + (gamma_new / gamma) * dir_snp
            gamma = gamma_new
    return sol_animal, sol_snp, res_animal, res_snp
```

```python
import functools
import types

import jax
import jax.numpy as jnp
from jax import lax
from jax.experimental import pallas as pl
from jax.experimental.pallas import tpu as pltpu
from jax.sharding import PartitionSpec as P

SPAN = 3
ITERS = 2
TRAITS = 4
HI = 256
OWN = 256
F32 = jnp.float32
BF16 = jnp.bfloat16
MESH = pl.DeviceIdType.MESH


def split(x):
    high = x.astype(BF16)
    return high, (x - high.astype(F32)).astype(BF16)


def mix(matrix, field):
    total = matrix[:, 0:1] * field[0:1, :]
    for u in range(1, TRAITS):
        total = total + matrix[:, u : u + 1] * field[u : u + 1, :]
    return total


def fold(x):
    total = x[:, 0:128]
    for i in range(1, x.shape[1] // 128):
        total = total + x[:, i * 128 : (i + 1) * 128]
    return jnp.sum(total, axis=0, keepdims=True)


def total_of(row):
    return jnp.sum(row, axis=1, keepdims=True)


def kernel(nc, nz, inputs, names, *refs):
    r = types.SimpleNamespace(**dict(zip(names, refs)))
    c = lax.axis_index("cohort")
    z = lax.axis_index("snp")
    slots = r.rhs_a.shape[1]
    part = slots // nz
    lows = slots // HI
    rows = lows * TRAITS
    prow = rows // nz
    snps = r.rhs_s.shape[1]
    genos = r.geno_idx.shape[1]
    owners = snps // OWN
    chunk = r.geno_f32.shape[2]
    chunks = snps // chunk
    own = lax.rem(c, owners)
    is_owner = c < owners
    own_at = pl.ds(pl.multiple_of(own * OWN, OWN), OWN)
    my_slots = pl.ds(pl.multiple_of(z * part, part), part)
    my_rows = pl.ds(pl.multiple_of(z * prow, prow), prow)

    def cohort_at(k):
        return lax.rem(c + k + nc, nc)

    def send(src, dst, send_sem, recv_sem, device):
        pltpu.make_async_remote_copy(
            src_ref=src, dst_ref=dst, send_sem=send_sem, recv_sem=recv_sem,
            device_id=device, device_id_type=MESH,
        ).start()

    def wait(ref, sem):
        pltpu.make_async_copy(ref, ref, sem).wait()

    loads = []
    for i, name in enumerate(inputs):
        loads.append(pltpu.make_async_copy(getattr(r, "in_" + name), getattr(r, name), r.load_sem.at[i]))
    for j in range(chunks):
        loads.append(
            pltpu.make_async_copy(
                r.in_genotypes.at[:, j * chunk : (j + 1) * chunk],
                r.geno_f32.at[j],
                r.load_sem.at[len(inputs) + j],
            )
        )
    for load in loads:
        load.start()

    barrier = pltpu.get_barrier_semaphore()

    @pl.loop(1, nz)
    def _(k):
        pl.semaphore_signal(barrier, inc=1, device_id=(c, lax.rem(z + k, nz)), device_id_type=MESH)

    @pl.loop(1, nc)
    def _(k):
        pl.semaphore_signal(barrier, inc=1, device_id=(cohort_at(k), z), device_id_type=MESH)

    for load in loads[: len(inputs)]:
        load.wait()

    r.idx_own[0:1, :] = r.sire[:, my_slots]
    r.idx_own[1:2, :] = r.dam[:, my_slots]

    pl.semaphore_wait(barrier, nz - 1 + nc - 1)

    for l in range(SPAN):
        send(
            r.idx_own, r.idx_recv.at[l], r.idx_ssem.at[l], r.idx_rsem.at[l],
            (cohort_at(-(l + 1)), z),
        )

    cohort_row = lax.broadcasted_iota(jnp.int32, (1, nc), 1)
    live_count = total_of(jnp.where(cohort_row == c, r.sizes[...].astype(F32), 0.0))

    @pl.loop(0, lows // 2)
    def _(j):
        here = pl.ds(pl.multiple_of(j * 2 * HI, 2 * HI), 2 * HI)
        slot = (lax.broadcasted_iota(jnp.int32, (1, 2 * HI), 1) + j * 2 * HI).astype(F32)
        res = jnp.where(slot < live_count, r.rhs_a[:, here], 0.0)
        r.res_a0[:, here] = res
        pre = r.pre_a[0, :, here] * res[0:1, :]
        for u in range(1, TRAITS):
            pre = pre + r.pre_a[u, :, here] * res[u : u + 1, :]
        r.z_a0[:, here] = pre
        r.field[0, pl.ds(pl.multiple_of(j * 8, 8), 8), :] = jnp.concatenate(
            [pre[:, :HI], pre[:, HI:]], axis=0
        )

    def precond_s(res, at):
        pre = r.pre_s[0, :, at] * res[0:1, :]
        for u in range(1, TRAITS):
            pre = pre + r.pre_s[u, :, at] * res[u : u + 1, :]
        return pre

    def precond_a(res):
        pre = r.pre_a[0, :, my_slots] * res[0:1, :]
        for u in range(1, TRAITS):
            pre = pre + r.pre_a[u, :, my_slots] * res[u : u + 1, :]
        return pre

    def marker_product(step, first):
        r.acc_m[...] = jnp.zeros_like(r.acc_m)
        if first:
            for load in loads[len(inputs) :]:
                load.wait()

        @pl.loop(0, chunks)
        def _(j):
            at = pl.ds(pl.multiple_of(j * chunk, chunk), chunk)
            if first:
                z_s = precond_s(r.rhs_s[:, at], at)
                r.z_s[0, :, at] = z_s
                high, low = split(r.geno_f32[j])
                r.geno_hi[j] = high
                r.geno_lo[j] = low
            else:
                z_s = r.z_s[step, :, at]
                high, low = r.geno_hi[j], r.geno_lo[j]
            s_high, s_low = split(z_s)
            both = jnp.concatenate([s_high.astype(F32), s_low.astype(F32)], axis=0).astype(BF16)
            dims = (((1,), (1,)), ((), ()))
            r.acc_m[...] += lax.dot_general(
                both, high, dims, preferred_element_type=F32
            ) + lax.dot_general(both, low, dims, preferred_element_type=F32)

        r.mk[step, z] = r.acc_m[0:TRAITS, :] + r.acc_m[TRAITS : 2 * TRAITS, :]

    first_animal = c * slots

    def one_hot(index):
        local = index - first_animal
        high = jnp.bitwise_and(local, HI - 1)
        low = jnp.right_shift(local, 8)
        n = index.shape[1]
        hot = (lax.broadcasted_iota(jnp.int32, (HI, n), 0) == high).astype(F32).astype(BF16)
        key = low - jnp.right_shift(lax.broadcasted_iota(jnp.int32, (8, n), 0), 2)
        return hot, key

    def gather(hot, key):
        picked = jnp.dot(r.field_bf[...], hot, preferred_element_type=F32)
        total = jnp.zeros((8, hot.shape[1]), F32)
        for g in range(rows // 8):
            value = picked[g * 8 : g * 8 + 8, :] + picked[rows + g * 8 : rows + g * 8 + 8, :]
            total = total + jnp.where(key == 2 * g, value, 0.0)
        return total[0:TRAITS, :] + total[TRAITS:8, :]

    def scatter(value, hot, key):
        twice = jnp.concatenate([value, value], axis=0)
        high, low = split(twice)
        pieces = []
        for piece in (high.astype(F32), low.astype(F32)):
            for g in range(rows // 8):
                pieces.append(jnp.where(key == 2 * g, piece, 0.0))
        spread = jnp.concatenate(pieces, axis=0).astype(BF16)
        r.acc_b[...] += lax.dot_general(
            spread, hot, (((1,), (1,)), ((), ())), preferred_element_type=F32
        )

    def to_snp(src_of, dst, send_sem, recv_sem):
        @pl.loop(1, nz)
        def _(k):
            other = lax.rem(z + k, nz)
            send(src_of(other), dst, send_sem, recv_sem, (c, other))

    def to_cohort(src, dst, send_sem, recv_sem):
        @pl.loop(1, nc)
        def _(k):
            send(src, dst, send_sem, recv_sem, (cohort_at(k), z))

    row4 = lax.broadcasted_iota(jnp.int32, (4, 128), 0)
    sire, dam = r.idx_own[0:1, :], r.idx_own[1:2, :]
    known = jnp.where(sire >= 0, 1.0, 0.0) + jnp.where(dam >= 0, 1.0, 0.0)
    factor = 4.0 / (4.0 - known)
    gen_inv, res_inv, coup, prior = (x[...] for x in (r.gen_inv, r.res_inv, r.coup, r.prior))
    at_z0 = jnp.where(z == 0, 1.0, 0.0)
    at_owner = jnp.where(is_owner, 1.0, 0.0)
    gamma0 = delta0 = alpha0 = None

    for step in range(ITERS):
        high, low = split(r.field[step])
        r.field_bf[0:rows, :] = high
        r.field_bf[rows : 2 * rows, :] = low

        if step == 0:
            marker_product(0, True)
            to_snp(lambda o: r.mk.at[0, z], r.mk.at[0, z], r.mk_ssem.at[0], r.mk_rsem.at[0])
            hot, key = one_hot(r.geno_idx[...])
            r.hot_g[...] = hot
            r.key_g[...] = key

        @pl.loop(0, SPAN)
        def _(l):
            if step == 0:
                wait(r.idx_recv.at[l], r.idx_rsem.at[l])
                for k in range(2):
                    hot, key = one_hot(r.idx_recv[l, k : k + 1, :])
                    r.hot[2 * l + k] = hot
                    r.key[2 * l + k] = key
            total = gather(r.hot[2 * l], r.key[2 * l])
            r.up_send[step, l] = total + gather(r.hot[2 * l + 1], r.key[2 * l + 1])
            send(
                r.up_send.at[step, l], r.up_recv.at[step, l],
                r.up_ssem.at[step, l], r.up_rsem.at[step, l], (cohort_at(l + 1), z),
            )

        if step > 0:
            @pl.when(is_owner)
            def _():
                wait(r.z_s.at[step, :, pl.ds(0, (owners - 1) * OWN)], r.zs_rsem)

            @pl.when(jnp.logical_not(is_owner))
            def _():
                wait(r.z_s.at[step], r.zs_rsem)

            marker_product(step, False)
            to_snp(
                lambda o: r.mk.at[step, z], r.mk.at[step, z],
                r.mk_ssem.at[step], r.mk_rsem.at[step],
            )
        dir_g = gather(r.hot_g[...], r.key_g[...])
        wait(r.mk.at[step, pl.ds(0, nz - 1)], r.mk_rsem.at[step])
        mismatch = dir_g - jnp.sum(r.mk[step], axis=0)
        tied = mix(coup, mismatch)

        t_high, t_low = split(tied)
        both = jnp.concatenate([t_high.astype(F32), t_low.astype(F32)], axis=0).astype(BF16)

        @pl.loop(0, chunks)
        def _(j):
            at = pl.ds(pl.multiple_of(j * chunk, chunk), chunk)
            sums = jnp.dot(both, r.geno_hi[j], preferred_element_type=F32) + jnp.dot(
                both, r.geno_lo[j], preferred_element_type=F32
            )
            r.part_s[step, :, at] = sums[0:TRAITS, :] + sums[TRAITS : 2 * TRAITS, :]

        r.sum_s[step, c] = r.part_s[step, :, own_at]

        @pl.loop(1, nc)
        def _(k):
            other = cohort_at(k)

            @pl.when(other < owners)
            def _():
                send(
                    r.part_s.at[step, :, pl.ds(pl.multiple_of(other * OWN, OWN), OWN)],
                    r.sum_s.at[step, c],
                    r.ss_ssem.at[step], r.ss_rsem.at[step], (other, z),
                )

        for l in range(SPAN):
            wait(r.up_recv.at[step, l], r.up_rsem.at[step, l])
        z_own = r.z_a0[:, my_slots] if step == 0 else r.z_own[...]
        parents = r.up_recv[step, 0] + r.up_recv[step, 1] + r.up_recv[step, 2]
        deviation = z_own - 0.5 * parents
        mixed = mix(gen_inv, factor * deviation)
        r.down_send[step] = mixed
        for l in range(SPAN):
            send(
                r.down_send.at[step], r.down_recv.at[step, l],
                r.down_ssem.at[step, l], r.down_rsem.at[step, l], (cohort_at(-(l + 1)), z),
            )
        own_image = r.weight[:, my_slots] * mix(res_inv, z_own)
        zs_own = r.z_s[step, :, own_at]
        prior_image = mix(prior, zs_own)
        curve = (
            fold(z_own * own_image + deviation * mixed)
            + at_z0 * fold(mismatch * tied)
            + at_owner * fold(zs_own * prior_image)
        )
        if step == 0:
            gamma_row = fold(z_own * r.res_a0[:, my_slots]) + at_owner * fold(
                zs_own * r.rhs_s[:, own_at]
            )
            cross_row = jnp.zeros((1, 128), F32)
        else:
            gamma_row, cross_row = gamma1_row, cross1_row
        r.dot_z[step, z] = jnp.where(
            row4 == 0, gamma_row, jnp.where(row4 == 1, curve, jnp.where(row4 == 2, cross_row, 0.0))
        )
        to_snp(
            lambda o: r.dot_z.at[step, z], r.dot_z.at[step, z],
            r.dz_ssem.at[step], r.dz_rsem.at[step],
        )

        r.acc_b[...] = jnp.zeros_like(r.acc_b)
        scatter(at_z0 * tied, r.hot_g[...], r.key_g[...])
        wait(r.dot_z.at[step, pl.ds(0, nz - 1)], r.dz_rsem.at[step])
        r.dot_c[step, c] = jnp.sum(r.dot_z[step], axis=0)
        to_cohort(
            r.dot_c.at[step, c], r.dot_c.at[step, c],
            r.dc_ssem.at[step], r.dc_rsem.at[step],
        )

        @pl.loop(0, SPAN)
        def _(l):
            wait(r.down_recv.at[step, l], r.down_rsem.at[step, l])
            value = -0.5 * r.down_recv[step, l]
            scatter(value, r.hot[2 * l], r.key[2 * l])
            scatter(value, r.hot[2 * l + 1], r.key[2 * l + 1])

        r.back[step] = r.acc_b[0:rows, :] + r.acc_b[rows : 2 * rows, :]
        r.back_recv[step, z] = r.back[step, my_rows, :]
        to_snp(
            lambda o: r.back.at[step, pl.ds(pl.multiple_of(o * prow, prow), prow), :],
            r.back_recv.at[step, z], r.bk_ssem.at[step], r.bk_rsem.at[step],
        )

        wait(r.dot_c.at[step, pl.ds(0, nc - 1)], r.dc_rsem.at[step])
        dots = jnp.sum(r.dot_c[step], axis=0)
        if step == 0:
            gamma0, delta0 = total_of(dots[0:1, :]), total_of(dots[1:2, :])
            alpha = alpha0 = gamma0 / delta0
            beta = None
        else:
            gamma1, delta_z, cross = (total_of(dots[i : i + 1, :]) for i in range(3))
            beta = gamma1 / gamma0
            alpha = gamma1 / (delta_z + 2.0 * beta * cross + beta * beta * delta0)

        @pl.when(is_owner)
        def _():
            wait(r.sum_s.at[step, pl.ds(0, nc - 1)], r.ss_rsem.at[step])

        image_s = prior_image - jnp.sum(jnp.where(is_owner, r.sum_s[step], 0.0), axis=0)
        if step == 0:
            res_s = r.rhs_s[:, own_at] - alpha * image_s
            r.image_s[...] = image_s
            r.res_s1[...] = res_s
            z_s = precond_s(res_s, own_at)
            target = r.z_s.at[1]
            sems = r.zs_ssem, r.zs_rsem
        else:
            z_s = r.res_s1[...] - alpha * (image_s + beta * r.image_s[...])
            target = r.rs_all
            sems = r.rs_ssem, r.rs_rsem

        @pl.when(is_owner)
        def _():
            target[:, own_at] = z_s
            to_cohort(target.at[:, own_at], target.at[:, own_at], *sems)

        if step == 0:
            gamma1_row = at_owner * fold(z_s * res_s)
            cross1_row = at_owner * fold(z_s * image_s)

        wait(r.back_recv.at[step, pl.ds(0, nz - 1)], r.bk_rsem.at[step])
        back = jnp.sum(r.back_recv[step], axis=0)
        back = jnp.concatenate([back[i : i + TRAITS, :] for i in range(0, prow, TRAITS)], axis=1)
        image_a = own_image + mixed + back
        if step == 0:
            res_a = r.res_a0[:, my_slots] - alpha * image_a
            z_a = precond_a(res_a)
            r.image_a[...] = image_a
            r.res_a1[...] = res_a
            r.z_own[...] = z_a
            for i in range(0, prow, 8):
                lo = i // TRAITS
                at = pl.ds(pl.multiple_of(z * prow + i, 8), 8)
                r.field[1, at, :] = jnp.concatenate(
                    [z_a[:, lo * HI : (lo + 1) * HI], z_a[:, (lo + 1) * HI : (lo + 2) * HI]], axis=0
                )
            mine = r.field.at[1, my_rows, :]
            to_snp(lambda o: mine, mine, r.fl_ssem, r.fl_rsem)
            gamma1_row = gamma1_row + fold(z_a * res_a)
            cross1_row = cross1_row + fold(z_a * image_a)
            wait(r.field.at[1, pl.ds(0, rows - prow), :], r.fl_rsem)
        else:
            r.ra_all[:, my_slots] = r.res_a1[...] - alpha * (image_a + beta * r.image_a[...])
            mine = r.ra_all.at[:, my_slots]
            to_snp(lambda o: mine, mine, r.ra_ssem, r.ra_rsem)

    start_part = alpha0 + alpha * beta

    @pl.loop(0, lows // 2)
    def _(j):
        here = pl.ds(pl.multiple_of(j * 2 * HI, 2 * HI), 2 * HI)
        z1 = r.field[1, pl.ds(pl.multiple_of(j * 8, 8), 8), :]
        z1 = jnp.concatenate([z1[0:TRAITS, :], z1[TRAITS:8, :]], axis=1)
        r.sol_a[:, here] = start_part * r.z_a0[:, here] + alpha * z1

    @pl.loop(0, owners)
    def _(j):
        here = pl.ds(pl.multiple_of(j * OWN, OWN), OWN)
        r.sol_s[:, here] = start_part * r.z_s[0, :, here] + alpha * r.z_s[1, :, here]

    @pl.when(is_owner)
    def _():
        wait(r.rs_all.at[:, pl.ds(0, (owners - 1) * OWN)], r.rs_rsem)

    @pl.when(jnp.logical_not(is_owner))
    def _():
        wait(r.rs_all, r.rs_rsem)

    r.out_rs[...] = r.rs_all[...]
    wait(r.ra_all.at[:, pl.ds(0, slots - part)], r.ra_rsem)
    r.out_ra[...] = r.ra_all[...]

    for l in range(SPAN):
        wait(r.idx_own, r.idx_ssem.at[l])
    for step in range(ITERS):
        for l in range(SPAN):
            wait(r.up_send.at[step, l], r.up_ssem.at[step, l])
            wait(r.down_send.at[step], r.down_ssem.at[step, l])
        wait(r.mk.at[step, pl.ds(0, nz - 1)], r.mk_ssem.at[step])
        wait(r.dot_z.at[step, pl.ds(0, nz - 1)], r.dz_ssem.at[step])
        wait(r.dot_c.at[step, pl.ds(0, nc - 1)], r.dc_ssem.at[step])
        wait(r.back_recv.at[step, pl.ds(0, nz - 1)], r.bk_ssem.at[step])

        @pl.when(is_owner)
        def _():
            wait(r.part_s.at[step, :, pl.ds(0, (owners - 1) * OWN)], r.ss_ssem.at[step])

        @pl.when(jnp.logical_not(is_owner))
        def _():
            wait(r.part_s.at[step], r.ss_ssem.at[step])

    @pl.when(is_owner)
    def _():
        wait(r.sum_s.at[0, pl.ds(0, nc - 1)], r.zs_ssem)
        wait(r.sum_s.at[1, pl.ds(0, nc - 1)], r.rs_ssem)

    wait(r.field.at[1, pl.ds(0, rows - prow), :], r.fl_ssem)
    wait(r.ra_all.at[:, pl.ds(0, slots - part)], r.ra_ssem)


def body(nc, nz, rhs_a, rhs_s, weight, sire, dam, sizes, geno_idx, genotypes, pre_a, pre_s, *small):
    slots, snps, genos = rhs_a.shape[1], rhs_s.shape[1], geno_idx.shape[0]
    part = slots // nz
    rows = slots // HI * TRAITS
    chunk = next(k for k in (1280, 1024, 512, 256) if snps % k == 0)
    chunks = snps // chunk
    vmem, dma = pltpu.VMEM, pltpu.SemaphoreType.DMA
    inputs = dict(
        rhs_a=rhs_a, rhs_s=rhs_s, weight=weight[None], sire=sire[None], dam=dam[None], sizes=sizes[None],
        geno_idx=geno_idx[None], pre_a=pre_a, pre_s=pre_s,
        gen_inv=small[0], res_inv=small[1], coup=small[2], prior=small[3],
    )
    scratch = {name: vmem(x.shape, x.dtype) for name, x in inputs.items()}
    scratch |= dict(
        geno_f32=vmem((chunks, genos, chunk), F32),
        geno_hi=vmem((chunks, genos, chunk), BF16),
        geno_lo=vmem((chunks, genos, chunk), BF16),
        idx_own=vmem((2, part), jnp.int32),
        idx_recv=vmem((SPAN, 2, part), jnp.int32),
        hot=vmem((2 * SPAN, HI, part), BF16),
        key=vmem((2 * SPAN, 8, part), jnp.int32),
        hot_g=vmem((HI, genos), BF16),
        key_g=vmem((8, genos), jnp.int32),
        res_a0=vmem((TRAITS, slots), F32),
        z_a0=vmem((TRAITS, slots), F32),
        field=vmem((ITERS, rows, HI), F32),
        field_bf=vmem((2 * rows, HI), BF16),
        z_s=vmem((ITERS, TRAITS, snps), F32),
        acc_m=vmem((2 * TRAITS, genos), F32),
        mk=vmem((ITERS, nz, TRAITS, genos), F32),
        part_s=vmem((ITERS, TRAITS, snps), F32),
        sum_s=vmem((ITERS, nc, TRAITS, OWN), F32),
        up_send=vmem((ITERS, SPAN, TRAITS, part), F32),
        up_recv=vmem((ITERS, SPAN, TRAITS, part), F32),
        down_send=vmem((ITERS, TRAITS, part), F32),
        down_recv=vmem((ITERS, SPAN, TRAITS, part), F32),
        dot_z=vmem((ITERS, nz, 4, 128), F32),
        dot_c=vmem((ITERS, nc, 4, 128), F32),
        acc_b=vmem((2 * rows, HI), F32),
        back=vmem((ITERS, rows, HI), F32),
        back_recv=vmem((ITERS, nz, rows // nz, HI), F32),
        image_a=vmem((TRAITS, part), F32),
        res_a1=vmem((TRAITS, part), F32),
        z_own=vmem((TRAITS, part), F32),
        image_s=vmem((TRAITS, OWN), F32),
        res_s1=vmem((TRAITS, OWN), F32),
        ra_all=vmem((TRAITS, slots), F32),
        rs_all=vmem((TRAITS, snps), F32),
        load_sem=dma((len(inputs) + chunks,)),
    )
    for name, shape in dict(
        idx=(SPAN,), up=(ITERS, SPAN), down=(ITERS, SPAN), mk=(ITERS,), ss=(ITERS,), dz=(ITERS,), dc=(ITERS,),
        bk=(ITERS,), zs=(), rs=(), fl=(), ra=(),
    ).items():
        scratch[name + "_ssem"] = dma(shape)
        scratch[name + "_rsem"] = dma(shape)
    names = ["in_" + name for name in inputs] + ["in_genotypes"]
    names += ["sol_a", "sol_s", "out_ra", "out_rs"] + list(scratch)
    outs = [jax.ShapeDtypeStruct(x.shape, F32) for x in (rhs_a, rhs_s, rhs_a, rhs_s)]
    return pl.pallas_call(
        functools.partial(kernel, nc, nz, list(inputs), names),
        out_shape=outs,
        in_specs=[pl.BlockSpec(memory_space=pl.ANY)] * (len(inputs) + 1),
        out_specs=[pl.BlockSpec(memory_space=pltpu.VMEM)] * 4,
        scratch_shapes=list(scratch.values()),
        compiler_params=pltpu.CompilerParams(
            collective_id=0, has_side_effects=True, vmem_limit_bytes=48 * 1024 * 1024
        ),
        cost_estimate=pl.CostEstimate(flops=4 * 10**9, bytes_accessed=10**7, transcendentals=0),
    )(*inputs.values(), genotypes)


def solution(mesh):
    nc, nz = mesh.shape["cohort"], mesh.shape["snp"]
    in_specs = (
        P(None, "cohort"),
        P(None, "snp"),
        P("cohort"),
        P("cohort"),
        P("cohort"),
        P(),
        P("cohort"),
        P("cohort", "snp"),
        P(None, None, "cohort"),
        P(None, None, "snp"),
        P(),
        P(),
        P(),
        P(),
    )
    out_specs = (P(None, "cohort"), P(None, "snp"), P(None, "cohort"), P(None, "snp"))
    return jax.shard_map(
        functools.partial(body, nc, nz), mesh=mesh, in_specs=in_specs, out_specs=out_specs, check_vma=False
    )
```

```python
import functools
import types

import jax
import jax.numpy as jnp
from jax import lax
from jax.experimental import pallas as pl
from jax.experimental.pallas import tpu as pltpu
from jax.sharding import PartitionSpec as P

SPAN = 3
TRAITS = 4
HI = 256
OWN = 256
F32 = jnp.float32
BF16 = jnp.bfloat16
MESH = pl.DeviceIdType.MESH


def split(x):
    high = x.astype(BF16)
    return high, (x - high.astype(F32)).astype(BF16)


def stacked_split(x):
    high, low = split(x)
    return jnp.concatenate([high.astype(F32), low.astype(F32)], axis=0).astype(BF16)


def mix(matrix, field):
    total = matrix[:, 0:1] * field[0:1, :]
    for u in range(1, TRAITS):
        total = total + matrix[:, u : u + 1] * field[u : u + 1, :]
    return total


def fold(x):
    total = x[:, 0:128]
    for i in range(1, x.shape[1] // 128):
        total = total + x[:, i * 128 : (i + 1) * 128]
    return jnp.sum(total, axis=0, keepdims=True)


def total_of(row):
    return jnp.sum(row, axis=1, keepdims=True)


def z_plan(nz):
    order = sorted(range(1, nz), key=lambda k: -min(k, nz - k))
    reach = nz // 4
    return order, reach, 2 * reach + 1 if nz >= 4 else nz


def kernel(nc, nz, names, *refs):
    r = types.SimpleNamespace(**dict(zip(names, refs)))
    c = lax.axis_index("cohort")
    z = lax.axis_index("snp")
    slots = r.rhs_a.shape[1]
    part = slots // nz
    lows = slots // HI
    rows = lows * TRAITS
    prow = rows // nz
    snps = r.rhs_s.shape[1]
    owners = snps // OWN
    chunk = r.geno_f32.shape[2]
    chunks = snps // chunk
    own_block = lax.rem(c, owners)
    is_owner = c < owners
    own_at = pl.ds(pl.multiple_of(own_block * OWN, OWN), OWN)
    my_slots = pl.ds(pl.multiple_of(z * part, part), part)
    order, reach, nears = z_plan(nz)
    near_rows = nears * prow
    far_rows = rows - near_rows
    my_rows = slice(reach * prow, (reach + 1) * prow)

    def cohort_at(k):
        return lax.rem(c + k + nc, nc)

    def send(src, dst, send_sem, recv_sem, device):
        pltpu.make_async_remote_copy(
            src_ref=src, dst_ref=dst, send_sem=send_sem, recv_sem=recv_sem,
            device_id=device, device_id_type=MESH,
        ).start()

    def wait(ref, sem):
        pltpu.make_async_copy(ref, ref, sem).wait()

    loads = []
    for src, dst in (
        (r.in_rhs_a, r.rhs_a),
        (r.in_pre_a, r.pre_a),
        (r.in_sizes, r.sizes),
        (r.in_geno_idx, r.geno_idx),
        (r.in_rhs_s, r.rhs_s),
        (r.in_pre_s, r.pre_s),
        (r.in_sire.at[:, my_slots], r.idx_own.at[0]),
        (r.in_dam.at[:, my_slots], r.idx_own.at[1]),
        (r.in_weight.at[:, my_slots], r.weight),
        (r.in_gen_inv, r.gen_inv),
        (r.in_res_inv, r.res_inv),
        (r.in_coup, r.coup),
        (r.in_prior, r.prior),
    ):
        loads.append(pltpu.make_async_copy(src, dst, r.load_sem.at[len(loads)]))
    for j in range(chunks):
        loads.append(
            pltpu.make_async_copy(
                r.in_genotypes.at[:, j * chunk : (j + 1) * chunk], r.geno_f32.at[j], r.load_sem.at[len(loads)]
            )
        )
    for load in loads:
        load.start()

    barrier = pltpu.get_barrier_semaphore()

    @pl.loop(1, nz)
    def _(k):
        pl.semaphore_signal(barrier, inc=1, device_id=(c, lax.rem(z + k, nz)), device_id_type=MESH)

    @pl.loop(1, nc)
    def _(k):
        pl.semaphore_signal(barrier, inc=1, device_id=(cohort_at(k), z), device_id_type=MESH)

    pl.semaphore_wait(barrier, nz - 1 + nc - 1)

    for l in range(SPAN):
        for k, src in enumerate((r.in_sire, r.in_dam)):
            send(
                src.at[:, my_slots], r.idx_recv.at[l, k], r.idx_ssem.at[l], r.idx_rsem.at[l],
                (cohort_at(-(l + 1)), z),
            )

    def to_snp(src_of, dst_of, send_sem, recv_sem_of, ks):
        for k in ks:
            send(src_of(k), dst_of(k), send_sem, recv_sem_of(k), (c, lax.rem(z + k, nz)))

    def around(act):
        ny = min(4, nc // 2)
        nx = nc // (2 * ny)
        x, y, core = c // (2 * ny), c // 2 % ny, c % 2

        @pl.loop(0, nc)
        def _(t):
            to_x = lax.rem(x + t // (2 * ny) + nx // 2, nx)
            to_y = lax.rem(y + t // 2 % ny + ny // 2, ny)
            other = (to_x * ny + to_y) * 2 + lax.rem(core + t, 2)
            pl.when(other != c)(lambda: act(other))

    def to_cohort(src, dst, send_sem, recv_sem):
        around(lambda other: send(src, dst, send_sem, recv_sem, (other, z)))

    for load in loads[:3]:
        load.wait()

    cohort_row = lax.broadcasted_iota(jnp.int32, (1, nc), 1)
    live_count = total_of(jnp.where(cohort_row == c, r.sizes[...].astype(F32), 0.0))

    def place_of(j):
        at = lax.rem(j + lows // 2 - z * (prow // 8) + reach * (prow // 8), lows // 2)
        return pl.ds(pl.multiple_of(at * 8, 8), 8)

    @pl.loop(0, lows // 2)
    def _(j):
        here = pl.ds(pl.multiple_of(j * 2 * HI, 2 * HI), 2 * HI)
        slot = (lax.broadcasted_iota(jnp.int32, (1, 2 * HI), 1) + j * 2 * HI).astype(F32)
        res = jnp.where(slot < live_count, r.rhs_a[:, here], 0.0)
        r.res_a0[:, here] = res
        pre = r.pre_a[0, :, here] * res[0:1, :]
        for u in range(1, TRAITS):
            pre = pre + r.pre_a[u, :, here] * res[u : u + 1, :]
        r.z_a0[:, here] = pre
        r.field[0, place_of(j), :] = jnp.concatenate([pre[:, :HI], pre[:, HI:]], axis=0)

    def precond_s(res, at):
        pre = r.pre_s[0, :, at] * res[0:1, :]
        for u in range(1, TRAITS):
            pre = pre + r.pre_s[u, :, at] * res[u : u + 1, :]
        return pre

    def precond_a(res):
        pre = r.pre_a[0, :, my_slots] * res[0:1, :]
        for u in range(1, TRAITS):
            pre = pre + r.pre_a[u, :, my_slots] * res[u : u + 1, :]
        return pre

    def marker_product(step):
        r.acc_m[...] = jnp.zeros_like(r.acc_m)

        @pl.loop(0, chunks)
        def _(j):
            at = pl.ds(pl.multiple_of(j * chunk, chunk), chunk)
            if step == 0:
                z_s = precond_s(r.rhs_s[:, at], at)
                r.z_s[0, :, at] = z_s
                high, low = split(r.geno_f32[j])
                r.geno_hi[j] = high
                r.geno_lo[j] = low
            else:
                z_s = r.z_s[step, :, at]
                high, low = r.geno_hi[j], r.geno_lo[j]
            both = stacked_split(z_s)
            dims = (((1,), (1,)), ((), ()))
            r.acc_m[...] += lax.dot_general(
                both, high, dims, preferred_element_type=F32
            ) + lax.dot_general(both, low, dims, preferred_element_type=F32)

        r.mk[step, z] = r.acc_m[0:TRAITS, :] + r.acc_m[TRAITS : 2 * TRAITS, :]
        mine = r.mk.at[step, z]
        to_snp(lambda k: mine, lambda k: mine, r.mk_ssem.at[step], lambda k: r.mk_rsem.at[step], order)

    first_animal = c * slots

    def one_hot(index):
        local = index - first_animal
        high = jnp.bitwise_and(local, HI - 1)
        low = jnp.right_shift(local, 8)
        n = index.shape[1]
        hot = (lax.broadcasted_iota(jnp.int32, (HI, n), 0) == high).astype(F32).astype(BF16)
        here = jnp.logical_and(low >= 0, low < lows)
        around_low = jnp.bitwise_and(low + (reach - z) * (lows // nz), lows - 1)
        place = jnp.where(here, around_low, -8)
        return hot, place - jnp.right_shift(lax.broadcasted_iota(jnp.int32, (8, n), 0), 2)

    near_part, far_part = (0, near_rows), (near_rows, far_rows)

    def load_field(step, which):
        first, count = which
        high, low = split(r.field[step, first : first + count, :])
        r.field_bf[2 * first : 2 * first + count, :] = high
        r.field_bf[2 * first + count : 2 * (first + count), :] = low

    def gather(which, hot, key):
        first, count = which
        picked = jnp.dot(
            r.field_bf[2 * first : 2 * (first + count), :], hot, preferred_element_type=F32
        )
        total = jnp.zeros((8, hot.shape[1]), F32)
        for g in range(count // 8):
            value = picked[g * 8 : g * 8 + 8, :] + picked[count + g * 8 : count + g * 8 + 8, :]
            total = total + jnp.where(key == 2 * (g + first // 8), value, 0.0)
        return total

    def gather_all(which, l):
        return gather(which, r.hot[2 * l], r.key[2 * l]) + gather(which, r.hot[2 * l + 1], r.key[2 * l + 1])

    def halves(total):
        return total[0:TRAITS, :] + total[TRAITS:8, :]

    def scatter(which, value, hot, key):
        first, count = which
        high, low = split(jnp.concatenate([value, value], axis=0))
        pieces = []
        for piece in (high.astype(F32), low.astype(F32)):
            for g in range(count // 8):
                pieces.append(jnp.where(key == 2 * (g + first // 8), piece, 0.0))
        spread = jnp.concatenate(pieces, axis=0).astype(BF16)
        return lax.dot_general(spread, hot, (((1,), (1,)), ((), ())), preferred_element_type=F32)

    def slots_of(block):
        return jnp.concatenate([block[i : i + TRAITS, :] for i in range(0, prow, TRAITS)], axis=1)

    readers = (((1, 0), (-1, 6), (-2, 8)), ((1, 1), (2, 3), (-1, 7)), ((1, 2), (2, 4), (3, 5)))

    def send_sums_up(step, l):
        def to(readers_l):
            for offset, place_there in readers_l:
                send(
                    r.up_own.at[step, l], r.up_recv.at[step, place_there],
                    r.up_ssem.at[step], r.up_rsem.at[step], (cohort_at(offset), z),
                )

        for i in range(SPAN):
            pl.when(l == i)(functools.partial(to, readers[i]))

    def send_own(step, src):
        for l in reversed(range(SPAN)):
            send(
                src, r.own_recv.at[step, l], r.own_ssem.at[step], r.own_rsem.at[step], (cohort_at(-(l + 1)), z)
            )

    def factor_of(sire, dam):
        known = jnp.where(sire >= 0, 1.0, 0.0) + jnp.where(dam >= 0, 1.0, 0.0)
        return 4.0 / (4.0 - known)

    row4 = lax.broadcasted_iota(jnp.int32, (4, 128), 0)
    at_owner = jnp.where(is_owner, 1.0, 0.0)
    every = (near_part, far_part) if far_rows else (near_part,)

    send_own(0, r.z_a0.at[:, my_slots])
    for load in loads[3:]:
        load.wait()
    gen_inv, res_inv, coup, prior = (x[...] for x in (r.gen_inv, r.res_inv, r.coup, r.prior))
    factor = factor_of(r.idx_own[0], r.idx_own[1])

    for step in range(2):
        if step == 0:
            marker_product(0)
            for which in every:
                load_field(0, which)

            @pl.loop(0, SPAN)
            def _(i):
                l = SPAN - 1 - i
                wait(r.idx_recv.at[l], r.idx_rsem.at[l])
                for k in range(2):
                    hot, key = one_hot(r.idx_recv[l, k])
                    r.hot[2 * l + k] = hot
                    r.key[2 * l + k] = key
                r.up_own[0, l] = halves(sum(gather_all(which, l) for which in every))
                send_sums_up(0, l)
                r.factor[l] = factor_of(r.idx_recv[l, 0], r.idx_recv[l, 1])

            hot, key = one_hot(r.geno_idx[...])
            r.hot_g[...] = hot
            r.key_g[...] = key
        else:
            if nears > 1:
                wait(r.field.at[1, pl.ds(0, near_rows - prow), :], r.fl_rsem.at[0])
            load_field(1, near_part)

            @pl.loop(0, SPAN)
            def _(l):
                r.partial[l] = gather_all(near_part, l)

            if far_rows:
                wait(r.field.at[1, near_rows:, :], r.fl_rsem.at[1])
                load_field(1, far_part)

            @pl.loop(0, SPAN)
            def _(i):
                l = SPAN - 1 - i
                total = r.partial[l]
                if far_rows:
                    total = total + gather_all(far_part, l)
                r.up_own[1, l] = halves(total)
                send_sums_up(1, l)

            @pl.when(is_owner)
            def _():
                wait(r.z_s.at[1, :, pl.ds(0, (owners - 1) * OWN)], r.zs_rsem)

            @pl.when(jnp.logical_not(is_owner))
            def _():
                wait(r.z_s.at[1], r.zs_rsem)

            marker_product(1)

            to_snp(
                lambda k: r.image_a, lambda k: r.q_a.at[:, my_slots], r.qa_ssem, lambda k: r.qa_rsem, order
            )
            r.q_a[:, my_slots] = r.image_a[...]

        dir_g = halves(sum(gather(which, r.hot_g[...], r.key_g[...]) for which in every))

        wait(r.own_recv.at[step], r.own_rsem.at[step])
        wait(r.up_recv.at[step], r.up_rsem.at[step])
        others = ((1, 4), (2, 6), (7, 8))
        for l in range(SPAN):
            parents = r.up_own[step, l] + r.up_recv[step, others[l][0]] + r.up_recv[step, others[l][1]]
            terms = r.factor[l] * (r.own_recv[step, l] - 0.5 * parents)
            r.terms[l] = -0.5 * mix(gen_inv, terms)
        r.acc_b[...] = jnp.zeros_like(r.acc_b)

        @pl.loop(0, SPAN)
        def _(l):
            r.acc_b[...] += scatter((0, rows), r.terms[l], r.hot[2 * l], r.key[2 * l]) + scatter(
                (0, rows), r.terms[l], r.hot[2 * l + 1], r.key[2 * l + 1]
            )

        r.back[step] = r.acc_b[0:rows, :] + r.acc_b[rows : 2 * rows, :]
        to_snp(
            lambda k: r.back.at[step, pl.ds((k + reach) % nz * prow, prow), :],
            lambda k: r.back_recv.at[step, k], r.bk_ssem.at[step], lambda k: r.bk_rsem.at[step], order,
        )
        r.back_recv[step, 0] = r.back[step, my_rows, :]

        own = r.z_a0[:, my_slots] if step == 0 else r.y_own[...]
        deviation = own - 0.5 * (r.up_recv[step, 0] + r.up_recv[step, 3] + r.up_recv[step, 5])
        mixed = mix(gen_inv, factor * deviation)
        local_a = r.weight[...] * mix(res_inv, own) + mixed
        own_s = r.z_s[step, :, own_at]
        local_s = mix(prior, own_s)
        if step == 0:
            r.local_s[...] = local_s
            r.deviation[...] = deviation
            curve = fold(own * (local_a - mixed) + deviation * mixed) + at_owner * fold(own_s * local_s)
            gamma_row = fold(own * r.res_a0[:, my_slots]) + at_owner * fold(own_s * r.rhs_s[:, own_at])
            cross_row = jnp.zeros((1, 128), F32)
        else:
            wait(r.dot_c.at[0, pl.ds(0, nc - 1)], r.dc_rsem.at[0])
            dots = jnp.sum(r.dot_c[0], axis=0)
            gamma0, delta0 = total_of(dots[0:1, :]), total_of(dots[1:2, :])
            alpha0 = gamma0 / delta0
            z_own = r.z_a0[:, my_slots] - alpha0 * own
            res_a1 = r.res_a0[:, my_slots] - alpha0 * r.image_a[...]
            zs_own = r.z_s[0, :, own_at] - alpha0 * own_s
            res_s1 = r.rhs_s[:, own_at] - alpha0 * r.image_s[...]
            gamma_row = fold(z_own * res_a1) + at_owner * fold(zs_own * res_s1)
            cross_row = fold(z_own * r.image_a[...]) + at_owner * fold(zs_own * r.image_s[...])
            deviation = r.deviation[...] - alpha0 * deviation
            z_mixed = mix(gen_inv, factor * deviation)
            record = r.weight[...] * mix(res_inv, z_own)
            curve = fold(z_own * record + deviation * z_mixed) + at_owner * fold(
                zs_own * (r.local_s[...] - alpha0 * local_s)
            )
        r.dot_z[step, z] = jnp.where(
            row4 == 0, gamma_row, jnp.where(row4 == 1, curve, jnp.where(row4 == 2, cross_row, 0.0))
        )
        my_dots = r.dot_z.at[step, z]
        to_snp(lambda k: my_dots, lambda k: my_dots, r.dz_ssem.at[step], lambda k: r.dz_rsem.at[step], order)

        wait(r.mk.at[step, pl.ds(0, nz - 1)], r.mk_rsem.at[step])
        mismatch = dir_g - jnp.sum(r.mk[step], axis=0)
        tied = mix(coup, mismatch)

        both = stacked_split(tied)

        @pl.loop(0, chunks)
        def _(j):
            at = pl.ds(pl.multiple_of(j * chunk, chunk), chunk)
            sums = jnp.dot(both, r.geno_hi[j], preferred_element_type=F32) + jnp.dot(
                both, r.geno_lo[j], preferred_element_type=F32
            )
            r.part_s[step, :, at] = sums[0:TRAITS, :] + sums[TRAITS : 2 * TRAITS, :]

        r.sum_s[step, c] = r.part_s[step, :, own_at]

        def send_sums(other):
            @pl.when(other < owners)
            def _():
                send(
                    r.part_s.at[step, :, pl.ds(pl.multiple_of(other * OWN, OWN), OWN)],
                    r.sum_s.at[step, c], r.ss_ssem.at[step], r.ss_rsem.at[step], (other, z),
                )

        around(send_sums)

        if step == 0:
            r.mismatch[...] = mismatch
            tied_row = fold(mismatch * tied)
        else:
            mismatch = r.mismatch[...] - alpha0 * mismatch
            tied_row = fold(mismatch * mix(coup, mismatch))
        wait(r.dot_z.at[step, pl.ds(0, nz - 1)], r.dz_rsem.at[step])
        r.dot_c[step, c] = jnp.sum(r.dot_z[step], axis=0) + jnp.where(row4 == 1, tied_row, 0.0)
        my_dots = r.dot_c.at[step, c]
        to_cohort(my_dots, my_dots, r.dc_ssem.at[step], r.dc_rsem.at[step])

        tie = scatter((reach * prow, prow), tied, r.hot_g[...], r.key_g[...])
        local_a = local_a + slots_of(tie[0:prow, :] + tie[prow : 2 * prow, :])
        wait(r.back_recv.at[step, pl.ds(0, nz - 1)], r.bk_rsem.at[step])
        image_a = local_a + slots_of(jnp.sum(r.back_recv[step], axis=0))
        if step == 0:
            y_a = precond_a(image_a)
            for i in range(0, prow, 8):
                lo = i // TRAITS
                at = reach * prow + i
                r.field[1, at : at + 8, :] = jnp.concatenate(
                    [y_a[:, lo * HI : (lo + 1) * HI], y_a[:, (lo + 1) * HI : (lo + 2) * HI]], axis=0
                )
            mine = r.field.at[1, my_rows, :]
            to_snp(
                lambda k: mine, lambda k: r.field.at[1, pl.ds((reach - k) % nz * prow, prow), :],
                r.fl_ssem, lambda k: r.fl_rsem.at[0 if (reach - k) % nz < nears else 1], order,
            )
            r.y_own[...] = y_a
            r.image_a[...] = image_a
            send_own(1, r.y_own)
        else:
            r.w_own[...] = image_a
            landing = r.w_a.at[:, my_slots]
            to_snp(lambda k: r.w_own, lambda k: landing, r.ra_ssem, lambda k: r.ra_rsem, order)
            r.w_a[:, my_slots] = image_a

        @pl.when(is_owner)
        def _():
            wait(r.sum_s.at[step, pl.ds(0, nc - 1)], r.ss_rsem.at[step])

        image_s = local_s - jnp.sum(jnp.where(is_owner, r.sum_s[step], 0.0), axis=0)
        if step == 0:
            r.image_s[...] = image_s
            y_s = precond_s(image_s, own_at)

            @pl.when(is_owner)
            def _():
                r.z_s[1, :, own_at] = y_s
                mine = r.z_s.at[1, :, own_at]
                to_cohort(mine, mine, r.zs_ssem, r.zs_rsem)
        else:

            @pl.when(is_owner)
            def _():
                r.w_s[:, own_at] = image_s
                mine = r.w_s.at[:, own_at]
                to_cohort(mine, mine, r.rs_ssem, r.rs_rsem)
                r.q_s[:, own_at] = r.image_s[...]
                mine = r.q_s.at[:, own_at]
                to_cohort(mine, mine, r.qs_ssem, r.qs_rsem)

    wait(r.dot_c.at[1, pl.ds(0, nc - 1)], r.dc_rsem.at[1])
    dots = jnp.sum(r.dot_c[1], axis=0)
    gamma1, delta_z, cross = (total_of(dots[i : i + 1, :]) for i in range(3))
    beta = gamma1 / gamma0
    alpha1 = gamma1 / (delta_z + 2.0 * beta * cross + beta * beta * delta0)

    once = alpha0 + alpha1 * (1.0 + beta)
    twice = alpha1 * alpha0
    wait(r.q_a.at[:, pl.ds(0, slots - part)], r.qa_rsem)
    wait(r.w_a.at[:, pl.ds(0, slots - part)], r.ra_rsem)

    @pl.loop(0, lows // 2)
    def _(j):
        here = pl.ds(pl.multiple_of(j * 2 * HI, 2 * HI), 2 * HI)
        y = r.field[1, place_of(j), :]
        y = jnp.concatenate([y[0:TRAITS, :], y[TRAITS:8, :]], axis=1)
        r.out_sol_a[:, here] = once * r.z_a0[:, here] - twice * y
        r.out_ra[:, here] = r.res_a0[:, here] - once * r.q_a[:, here] + twice * r.w_a[:, here]

    for full, sem in ((r.q_s, r.qs_rsem), (r.w_s, r.rs_rsem)):

        @pl.when(is_owner)
        def _():
            wait(full.at[:, pl.ds(0, (owners - 1) * OWN)], sem)

        @pl.when(jnp.logical_not(is_owner))
        def _():
            wait(full, sem)

    @pl.loop(0, owners)
    def _(j):
        here = pl.ds(pl.multiple_of(j * OWN, OWN), OWN)
        r.out_sol_s[:, here] = once * r.z_s[0, :, here] - twice * r.z_s[1, :, here]
        r.out_rs[:, here] = r.rhs_s[:, here] - once * r.q_s[:, here] + twice * r.w_s[:, here]

    for l in range(SPAN):
        wait(r.idx_own, r.idx_ssem.at[l])
    for step in range(2):
        wait(r.up_recv.at[step], r.up_ssem.at[step])
        wait(r.own_recv.at[step], r.own_ssem.at[step])
        wait(r.mk.at[step, pl.ds(0, nz - 1)], r.mk_ssem.at[step])
        wait(r.dot_z.at[step, pl.ds(0, nz - 1)], r.dz_ssem.at[step])
        wait(r.dot_c.at[step, pl.ds(0, nc - 1)], r.dc_ssem.at[step])
        wait(r.back_recv.at[step, pl.ds(0, nz - 1)], r.bk_ssem.at[step])

        @pl.when(is_owner)
        def _():
            wait(r.part_s.at[step, :, pl.ds(0, (owners - 1) * OWN)], r.ss_ssem.at[step])

        @pl.when(jnp.logical_not(is_owner))
        def _():
            wait(r.part_s.at[step], r.ss_ssem.at[step])

    @pl.when(is_owner)
    def _():
        for sem in (r.zs_ssem, r.qs_ssem, r.rs_ssem):
            wait(r.sum_s.at[0, pl.ds(0, nc - 1)], sem)

    wait(r.field.at[1, pl.ds(0, rows - prow), :], r.fl_ssem)
    wait(r.q_a.at[:, pl.ds(0, slots - part)], r.qa_ssem)
    wait(r.w_a.at[:, pl.ds(0, slots - part)], r.ra_ssem)


def place(*refs):
    half = len(refs) // 2
    for i in range(half):
        refs[half + i][...] = refs[i][...]


def body(nc, nz, rhs_a, rhs_s, weight, sire, dam, sizes, geno_idx, genotypes, pre_a, pre_s, *small):
    slots, snps, genos = rhs_a.shape[1], rhs_s.shape[1], geno_idx.shape[0]
    part = slots // nz
    rows = slots // HI * TRAITS
    chunk = next(k for k in (1280, 1024, 512, 256) if snps % k == 0)
    chunks = snps // chunk
    vmem, dma = pltpu.VMEM, pltpu.SemaphoreType.DMA
    inputs = dict(
        rhs_a=rhs_a, rhs_s=rhs_s, weight=weight[None], sire=sire[None], dam=dam[None], sizes=sizes[None],
        geno_idx=geno_idx[None], genotypes=genotypes, pre_a=pre_a, pre_s=pre_s,
        gen_inv=small[0], res_inv=small[1], coup=small[2], prior=small[3],
    )
    scratch = dict(
        rhs_a=vmem(rhs_a.shape, F32),
        rhs_s=vmem(rhs_s.shape, F32),
        weight=vmem((1, part), F32),
        sizes=vmem((1, nc), jnp.int32),
        geno_idx=vmem((1, genos), jnp.int32),
        pre_a=vmem(pre_a.shape, F32),
        pre_s=vmem(pre_s.shape, F32),
        gen_inv=vmem((TRAITS, TRAITS), F32),
        res_inv=vmem((TRAITS, TRAITS), F32),
        coup=vmem((TRAITS, TRAITS), F32),
        prior=vmem((TRAITS, TRAITS), F32),
        geno_f32=vmem((chunks, genos, chunk), F32),
        geno_hi=vmem((chunks, genos, chunk), BF16),
        geno_lo=vmem((chunks, genos, chunk), BF16),
        idx_own=vmem((2, 1, part), jnp.int32),
        idx_recv=vmem((SPAN, 2, 1, part), jnp.int32),
        hot=vmem((2 * SPAN, HI, part), BF16),
        key=vmem((2 * SPAN, 8, part), jnp.int32),
        hot_g=vmem((HI, genos), BF16),
        key_g=vmem((8, genos), jnp.int32),
        res_a0=vmem((TRAITS, slots), F32),
        z_a0=vmem((TRAITS, slots), F32),
        field=vmem((2, rows, HI), F32),
        field_bf=vmem((2 * rows, HI), BF16),
        partial=vmem((SPAN, 8, part), F32),
        z_s=vmem((2, TRAITS, snps), F32),
        acc_m=vmem((2 * TRAITS, genos), F32),
        mk=vmem((2, nz, TRAITS, genos), F32),
        part_s=vmem((2, TRAITS, snps), F32),
        sum_s=vmem((2, nc, TRAITS, OWN), F32),
        factor=vmem((SPAN, 1, part), F32),
        up_own=vmem((2, SPAN, TRAITS, part), F32),
        up_recv=vmem((2, 9, TRAITS, part), F32),
        own_recv=vmem((2, SPAN, TRAITS, part), F32),
        terms=vmem((SPAN, TRAITS, part), F32),
        dot_z=vmem((2, nz, 4, 128), F32),
        dot_c=vmem((2, nc, 4, 128), F32),
        acc_b=vmem((2 * rows, HI), F32),
        back=vmem((2, rows, HI), F32),
        back_recv=vmem((2, nz, rows // nz, HI), F32),
        image_a=vmem((TRAITS, part), F32),
        y_own=vmem((TRAITS, part), F32),
        w_own=vmem((TRAITS, part), F32),
        deviation=vmem((TRAITS, part), F32),
        mismatch=vmem((TRAITS, genos), F32),
        local_s=vmem((TRAITS, OWN), F32),
        image_s=vmem((TRAITS, OWN), F32),
        q_a=vmem((TRAITS, slots), F32),
        w_a=vmem((TRAITS, slots), F32),
        q_s=vmem((TRAITS, snps), F32),
        w_s=vmem((TRAITS, snps), F32),
        load_sem=dma((13 + chunks,)),
    )
    for name, shape in dict(
        idx=(SPAN,), up=(2,), own=(2,), mk=(2,), ss=(2,), dz=(2,), dc=(2,), bk=(2,), zs=(), rs=(), qs=(), qa=(), ra=(),
    ).items():
        scratch[name + "_ssem"] = dma(shape)
        scratch[name + "_rsem"] = dma(shape)
    scratch |= dict(fl_ssem=dma(()), fl_rsem=dma((2,)))
    names = ["in_" + name for name in inputs]
    names += ["out_sol_a", "out_sol_s", "out_ra", "out_rs"] + list(scratch)
    outs = [jax.ShapeDtypeStruct(x.shape, F32) for x in (rhs_a, rhs_s, rhs_a, rhs_s)]
    limit = 56 * 1024 * 1024
    results = pl.pallas_call(
        functools.partial(kernel, nc, nz, names),
        out_shape=outs,
        in_specs=[pl.BlockSpec(memory_space=pl.ANY)] * len(inputs),
        out_specs=[pl.BlockSpec(memory_space=pltpu.VMEM)] * 4,
        scratch_shapes=list(scratch.values()),
        compiler_params=pltpu.CompilerParams(collective_id=0, has_side_effects=True, vmem_limit_bytes=limit),
        cost_estimate=pl.CostEstimate(flops=4 * 10**9, bytes_accessed=10**7, transcendentals=0),
    )(*inputs.values())
    return pl.pallas_call(
        place,
        out_shape=outs,
        in_specs=[pl.BlockSpec(memory_space=pltpu.VMEM)] * 4,
        out_specs=[pl.BlockSpec(memory_space=pltpu.VMEM)] * 4,
    )(*results)


def solution(mesh):
    nc, nz = mesh.shape["cohort"], mesh.shape["snp"]
    in_specs = (
        P(None, "cohort"),
        P(None, "snp"),
        P("cohort"),
        P("cohort"),
        P("cohort"),
        P(),
        P("cohort"),
        P("cohort", "snp"),
        P(None, None, "cohort"),
        P(None, None, "snp"),
        P(),
        P(),
        P(),
        P(),
    )
    out_specs = (P(None, "cohort"), P(None, "snp"), P(None, "cohort"), P(None, "snp"))
    return jax.shard_map(
        functools.partial(body, nc, nz), mesh=mesh, in_specs=in_specs, out_specs=out_specs, check_vma=False
    )
```

```python
import functools
import types

import jax
import jax.numpy as jnp
from jax import lax
from jax.experimental import pallas as pl
from jax.experimental.pallas import tpu as pltpu
from jax.sharding import PartitionSpec as P

SPAN = 3
TRAITS = 4
HI = 256
OWN = 256
F32 = jnp.float32
BF16 = jnp.bfloat16
MESH = pl.DeviceIdType.MESH


def split(x):
    high = x.astype(BF16)
    return high, (x - high.astype(F32)).astype(BF16)


def stacked_split(x):
    high, low = split(x)
    return jnp.concatenate([high.astype(F32), low.astype(F32)], axis=0).astype(BF16)


def mix(matrix, field):
    total = matrix[:, 0:1] * field[0:1, :]
    for u in range(1, TRAITS):
        total = total + matrix[:, u : u + 1] * field[u : u + 1, :]
    return total


def fold(x):
    total = x[:, 0:128]
    for i in range(1, x.shape[1] // 128):
        total = total + x[:, i * 128 : (i + 1) * 128]
    return jnp.sum(total, axis=0, keepdims=True)


def total_of(row):
    return jnp.sum(row, axis=1, keepdims=True)


def z_plan(nz):
    order = sorted(range(1, nz), key=lambda k: -min(k, nz - k))
    reach = nz // 4
    return order, reach, 2 * reach + 1 if nz >= 4 else nz


def kernel(nc, nz, names, *refs):
    r = types.SimpleNamespace(**dict(zip(names, refs)))
    c = lax.axis_index("cohort")
    z = lax.axis_index("snp")
    slots = r.rhs_a.shape[1]
    part = slots // nz
    lows = slots // HI
    rows = lows * TRAITS
    prow = rows // nz
    snps = r.rhs_s.shape[1]
    owners = snps // OWN
    chunk = r.geno_f32.shape[2]
    chunks = snps // chunk
    own_block = lax.rem(c, owners)
    is_owner = c < owners
    own_at = pl.ds(pl.multiple_of(own_block * OWN, OWN), OWN)
    my_slots = pl.ds(pl.multiple_of(z * part, part), part)
    order, reach, nears = z_plan(nz)
    near_rows = nears * prow
    far_rows = rows - near_rows
    my_rows = slice(reach * prow, (reach + 1) * prow)

    def cohort_at(k):
        return lax.rem(c + k + nc, nc)

    def send(src, dst, send_sem, recv_sem, device):
        pltpu.make_async_remote_copy(
            src_ref=src, dst_ref=dst, send_sem=send_sem, recv_sem=recv_sem,
            device_id=device, device_id_type=MESH,
        ).start()

    def wait(ref, sem):
        pltpu.make_async_copy(ref, ref, sem).wait()

    loads = []
    for src, dst in (
        (r.in_rhs_a, r.rhs_a),
        (r.in_pre_a, r.pre_a),
        (r.in_sizes, r.sizes),
        (r.in_geno_idx, r.geno_idx),
        (r.in_rhs_s, r.rhs_s),
        (r.in_pre_s, r.pre_s),
        (r.in_sire.at[:, my_slots], r.idx_own.at[0]),
        (r.in_dam.at[:, my_slots], r.idx_own.at[1]),
        (r.in_weight.at[:, my_slots], r.weight),
        (r.in_gen_inv, r.gen_inv),
        (r.in_res_inv, r.res_inv),
        (r.in_coup, r.coup),
        (r.in_prior, r.prior),
    ):
        loads.append(pltpu.make_async_copy(src, dst, r.load_sem.at[len(loads)]))
    for j in range(chunks):
        loads.append(
            pltpu.make_async_copy(
                r.in_genotypes.at[:, j * chunk : (j + 1) * chunk], r.geno_f32.at[j], r.load_sem.at[len(loads)]
            )
        )
    for load in loads:
        load.start()

    barrier = pltpu.get_barrier_semaphore()

    @pl.loop(1, nz)
    def _(k):
        pl.semaphore_signal(barrier, inc=1, device_id=(c, lax.rem(z + k, nz)), device_id_type=MESH)

    @pl.loop(1, nc)
    def _(k):
        pl.semaphore_signal(barrier, inc=1, device_id=(cohort_at(k), z), device_id_type=MESH)

    pl.semaphore_wait(barrier, nz - 1 + nc - 1)

    for l in range(SPAN):
        for k, src in enumerate((r.in_sire, r.in_dam)):
            send(
                src.at[:, my_slots], r.idx_recv.at[l, k], r.idx_ssem.at[l], r.idx_rsem.at[l],
                (cohort_at(-(l + 1)), z),
            )

    def to_snp(src_of, dst_of, send_sem, recv_sem_of, ks):
        for k in ks:
            send(src_of(k), dst_of(k), send_sem, recv_sem_of(k), (c, lax.rem(z + k, nz)))

    def around(act):
        ny = min(4, nc // 2)
        nx = nc // (2 * ny)
        x, y, core = c // (2 * ny), c // 2 % ny, c % 2
        xs = [lax.rem(x + (i + nx // 2) % nx, nx) * (2 * ny) for i in range(nx)]
        ys = [lax.rem(y + (i + ny // 2) % ny, ny) * 2 for i in range(ny)]
        cores = [core, 1 - core]
        for i in range(nx):
            for j in range(ny):
                for k in range(2):
                    if (i + nx // 2) % nx or (j + ny // 2) % ny or k:
                        act(xs[i] + ys[j] + cores[k])

    def to_cohort(src, dst, send_sem, recv_sem):
        around(lambda other: send(src, dst, send_sem, recv_sem, (other, z)))

    for load in loads[:3]:
        load.wait()

    cohort_row = lax.broadcasted_iota(jnp.int32, (1, nc), 1)
    live_count = total_of(jnp.where(cohort_row == c, r.sizes[...].astype(F32), 0.0))

    def place_of(j):
        at = lax.rem(j + lows // 2 - z * (prow // 8) + reach * (prow // 8), lows // 2)
        return pl.ds(pl.multiple_of(at * 8, 8), 8)

    @pl.loop(0, lows // 2, unroll=4)
    def _(j):
        here = pl.ds(pl.multiple_of(j * 2 * HI, 2 * HI), 2 * HI)
        slot = (lax.broadcasted_iota(jnp.int32, (1, 2 * HI), 1) + j * 2 * HI).astype(F32)
        res = jnp.where(slot < live_count, r.rhs_a[:, here], 0.0)
        r.res_a0[:, here] = res
        pre = r.pre_a[0, :, here] * res[0:1, :]
        for u in range(1, TRAITS):
            pre = pre + r.pre_a[u, :, here] * res[u : u + 1, :]
        r.z_a0[:, here] = pre
        r.field[0, place_of(j), :] = jnp.concatenate([pre[:, :HI], pre[:, HI:]], axis=0)

    def precond_s(res, at):
        pre = r.pre_s[0, :, at] * res[0:1, :]
        for u in range(1, TRAITS):
            pre = pre + r.pre_s[u, :, at] * res[u : u + 1, :]
        return pre

    def precond_a(res):
        pre = r.pre_a[0, :, my_slots] * res[0:1, :]
        for u in range(1, TRAITS):
            pre = pre + r.pre_a[u, :, my_slots] * res[u : u + 1, :]
        return pre

    def marker_product(step):
        r.acc_m[...] = jnp.zeros_like(r.acc_m)

        @pl.loop(0, chunks)
        def _(j):
            at = pl.ds(pl.multiple_of(j * chunk, chunk), chunk)
            if step == 0:
                z_s = precond_s(r.rhs_s[:, at], at)
                r.z_s[0, :, at] = z_s
                high, low = split(r.geno_f32[j])
                r.geno_hi[j] = high
                r.geno_lo[j] = low
            else:
                z_s = r.z_s[step, :, at]
                high, low = r.geno_hi[j], r.geno_lo[j]
            both = stacked_split(z_s)
            dims = (((1,), (1,)), ((), ()))
            r.acc_m[...] += lax.dot_general(
                both, high, dims, preferred_element_type=F32
            ) + lax.dot_general(both, low, dims, preferred_element_type=F32)

        r.mk[step, z] = r.acc_m[0:TRAITS, :] + r.acc_m[TRAITS : 2 * TRAITS, :]
        mine = r.mk.at[step, z]
        to_snp(lambda k: mine, lambda k: mine, r.mk_ssem.at[step], lambda k: r.mk_rsem.at[step], order)

    first_animal = c * slots

    def one_hot(index):
        local = index - first_animal
        high = jnp.bitwise_and(local, HI - 1)
        low = jnp.right_shift(local, 8)
        n = index.shape[1]
        hot = (lax.broadcasted_iota(jnp.int32, (HI, n), 0) == high).astype(F32).astype(BF16)
        here = jnp.logical_and(low >= 0, low < lows)
        around_low = jnp.bitwise_and(low + (reach - z) * (lows // nz), lows - 1)
        place = jnp.where(here, around_low, -8)
        return hot, place - jnp.right_shift(lax.broadcasted_iota(jnp.int32, (8, n), 0), 2)

    near_part, far_part = (0, near_rows), (near_rows, far_rows)

    def load_field(step, which):
        first, count = which
        high, low = split(r.field[step, first : first + count, :])
        r.field_bf[2 * first : 2 * first + count, :] = high
        r.field_bf[2 * first + count : 2 * (first + count), :] = low

    def gather(which, hot, key):
        first, count = which
        picked = jnp.dot(
            r.field_bf[2 * first : 2 * (first + count), :], hot, preferred_element_type=F32
        )
        total = jnp.zeros((8, hot.shape[1]), F32)
        for g in range(count // 8):
            value = picked[g * 8 : g * 8 + 8, :] + picked[count + g * 8 : count + g * 8 + 8, :]
            total = total + jnp.where(key == 2 * (g + first // 8), value, 0.0)
        return total

    def gather_all(which, l):
        return gather(which, r.hot[2 * l], r.key[2 * l]) + gather(which, r.hot[2 * l + 1], r.key[2 * l + 1])

    def halves(total):
        return total[0:TRAITS, :] + total[TRAITS:8, :]

    def scatter(which, value, hot, key):
        first, count = which
        high, low = split(jnp.concatenate([value, value], axis=0))
        pieces = []
        for piece in (high.astype(F32), low.astype(F32)):
            for g in range(count // 8):
                pieces.append(jnp.where(key == 2 * (g + first // 8), piece, 0.0))
        spread = jnp.concatenate(pieces, axis=0).astype(BF16)
        return lax.dot_general(spread, hot, (((1,), (1,)), ((), ())), preferred_element_type=F32)

    def slots_of(block):
        return jnp.concatenate([block[i : i + TRAITS, :] for i in range(0, prow, TRAITS)], axis=1)

    readers = (((1, 0), (-1, 6), (-2, 8)), ((1, 1), (2, 3), (-1, 7)), ((1, 2), (2, 4), (3, 5)))

    def send_sums_up(step, l):
        def to(readers_l):
            for offset, place_there in readers_l:
                send(
                    r.up_own.at[step, l], r.up_recv.at[step, place_there],
                    r.up_ssem.at[step], r.up_rsem.at[step], (cohort_at(offset), z),
                )

        if isinstance(l, int):
            to(readers[l])
        else:
            for i in range(SPAN):
                pl.when(l == i)(functools.partial(to, readers[i]))

    def send_own(step, src):
        for l in reversed(range(SPAN)):
            send(
                src, r.own_recv.at[step, l], r.own_ssem.at[step], r.own_rsem.at[step], (cohort_at(-(l + 1)), z)
            )

    def factor_of(sire, dam):
        known = jnp.where(sire >= 0, 1.0, 0.0) + jnp.where(dam >= 0, 1.0, 0.0)
        return 4.0 / (4.0 - known)

    row4 = lax.broadcasted_iota(jnp.int32, (4, 128), 0)
    at_owner = jnp.where(is_owner, 1.0, 0.0)
    every = (near_part, far_part) if far_rows else (near_part,)
    whole = (0, rows)

    send_own(0, r.z_a0.at[:, my_slots])
    for load in loads[3:]:
        load.wait()
    gen_inv, res_inv, coup, prior = (x[...] for x in (r.gen_inv, r.res_inv, r.coup, r.prior))
    factor = factor_of(r.idx_own[0], r.idx_own[1])

    for step in range(2):
        if step == 0:
            marker_product(0)
            load_field(0, whole)

            @pl.loop(0, SPAN)
            def _(i):
                l = SPAN - 1 - i
                wait(r.idx_recv.at[l], r.idx_rsem.at[l])
                for k in range(2):
                    hot, key = one_hot(r.idx_recv[l, k])
                    r.hot[2 * l + k] = hot
                    r.key[2 * l + k] = key
                r.up_own[0, l] = halves(gather_all(whole, l))
                send_sums_up(0, l)
                r.factor[l] = factor_of(r.idx_recv[l, 0], r.idx_recv[l, 1])

            hot, key = one_hot(r.geno_idx[...])
            r.hot_g[...] = hot
            r.key_g[...] = key
        else:
            if nears > 1:
                wait(r.field.at[1, pl.ds(0, near_rows - prow), :], r.fl_rsem.at[0])
            load_field(1, near_part)

            for l in range(SPAN):
                r.partial[l] = gather_all(near_part, l)

            if far_rows:
                wait(r.field.at[1, near_rows:, :], r.fl_rsem.at[1])
                load_field(1, far_part)

            for l in reversed(range(SPAN)):
                total = r.partial[l]
                if far_rows:
                    total = total + gather_all(far_part, l)
                r.up_own[1, l] = halves(total)
                send_sums_up(1, l)

            @pl.when(is_owner)
            def _():
                wait(r.z_s.at[1, :, pl.ds(0, (owners - 1) * OWN)], r.zs_rsem)

            @pl.when(jnp.logical_not(is_owner))
            def _():
                wait(r.z_s.at[1], r.zs_rsem)

            marker_product(1)

            to_snp(
                lambda k: r.image_a, lambda k: r.q_a.at[:, my_slots], r.qa_ssem, lambda k: r.qa_rsem, order
            )
            r.q_a[:, my_slots] = r.image_a[...]

            @pl.when(is_owner)
            def _():
                r.q_s[:, own_at] = r.image_s[...]
                mine = r.q_s.at[:, own_at]
                to_cohort(mine, mine, r.qs_ssem, r.qs_rsem)

        dir_g = halves(sum(gather(which, r.hot_g[...], r.key_g[...]) for which in (every if step else (whole,))))

        def tie_up():
            wait(r.mk.at[step, pl.ds(0, nz - 1)], r.mk_rsem.at[step])
            mismatch = dir_g - jnp.sum(r.mk[step], axis=0)
            tied = mix(coup, mismatch)

            both = stacked_split(tied)

            @pl.loop(0, chunks)
            def _(j):
                at = pl.ds(pl.multiple_of(j * chunk, chunk), chunk)
                sums = jnp.dot(both, r.geno_hi[j], preferred_element_type=F32) + jnp.dot(
                    both, r.geno_lo[j], preferred_element_type=F32
                )
                r.part_s[step, :, at] = sums[0:TRAITS, :] + sums[TRAITS : 2 * TRAITS, :]

            r.sum_s[step, c] = r.part_s[step, :, own_at]

            def send_sums(other):
                @pl.when(other < owners)
                def _():
                    send(
                        r.part_s.at[step, :, pl.ds(pl.multiple_of(other * OWN, OWN), OWN)],
                        r.sum_s.at[step, c], r.ss_ssem.at[step], r.ss_rsem.at[step], (other, z),
                    )

            around(send_sums)
            return mismatch, tied

        if step == 0:
            mismatch, tied = tie_up()

        wait(r.own_recv.at[step], r.own_rsem.at[step])
        wait(r.up_recv.at[step], r.up_rsem.at[step])
        own = r.z_a0[:, my_slots] if step == 0 else r.y_own[...]
        deviation = own - 0.5 * (r.up_recv[step, 0] + r.up_recv[step, 3] + r.up_recv[step, 5])
        mixed = mix(gen_inv, factor * deviation)
        local_a = r.weight[...] * mix(res_inv, own) + mixed
        own_s = r.z_s[step, :, own_at]
        local_s = mix(prior, own_s)
        if step == 0:
            r.local_s[...] = local_s
            r.deviation[...] = deviation
            curve = fold(own * (local_a - mixed) + deviation * mixed) + at_owner * fold(own_s * local_s)
            gamma_row = fold(own * r.res_a0[:, my_slots]) + at_owner * fold(own_s * r.rhs_s[:, own_at])
            cross_row = jnp.zeros((1, 128), F32)
        else:
            wait(r.dot_c.at[0, pl.ds(0, nc - 1)], r.dc_rsem.at[0])
            dots = jnp.sum(r.dot_c[0], axis=0)
            gamma0, delta0 = total_of(dots[0:1, :]), total_of(dots[1:2, :])
            alpha0 = gamma0 / delta0
            z_own = r.z_a0[:, my_slots] - alpha0 * own
            res_a1 = r.res_a0[:, my_slots] - alpha0 * r.image_a[...]
            zs_own = r.z_s[0, :, own_at] - alpha0 * own_s
            res_s1 = r.rhs_s[:, own_at] - alpha0 * r.image_s[...]
            gamma_row = fold(z_own * res_a1) + at_owner * fold(zs_own * res_s1)
            cross_row = fold(z_own * r.image_a[...]) + at_owner * fold(zs_own * r.image_s[...])
            deviation = r.deviation[...] - alpha0 * deviation
            z_mixed = mix(gen_inv, factor * deviation)
            record = r.weight[...] * mix(res_inv, z_own)
            curve = fold(z_own * record + deviation * z_mixed) + at_owner * fold(
                zs_own * (r.local_s[...] - alpha0 * local_s)
            )
        r.dot_z[step, z] = jnp.where(
            row4 == 0, gamma_row, jnp.where(row4 == 1, curve, jnp.where(row4 == 2, cross_row, 0.0))
        )
        my_dots = r.dot_z.at[step, z]
        to_snp(lambda k: my_dots, lambda k: my_dots, r.dz_ssem.at[step], lambda k: r.dz_rsem.at[step], order)

        others = ((1, 4), (2, 6), (7, 8))
        for l in range(SPAN):
            parents = r.up_own[step, l] + r.up_recv[step, others[l][0]] + r.up_recv[step, others[l][1]]
            terms = r.factor[l] * (r.own_recv[step, l] - 0.5 * parents)
            r.terms[l] = -0.5 * mix(gen_inv, terms)
        r.acc_b[...] = jnp.zeros_like(r.acc_b)

        @pl.loop(0, SPAN)
        def _(l):
            r.acc_b[...] += scatter(whole, r.terms[l], r.hot[2 * l], r.key[2 * l]) + scatter(
                whole, r.terms[l], r.hot[2 * l + 1], r.key[2 * l + 1]
            )

        r.back[step] = r.acc_b[0:rows, :] + r.acc_b[rows : 2 * rows, :]
        to_snp(
            lambda k: r.back.at[step, pl.ds((k + reach) % nz * prow, prow), :],
            lambda k: r.back_recv.at[step, k], r.bk_ssem.at[step], lambda k: r.bk_rsem.at[step], order,
        )
        r.back_recv[step, 0] = r.back[step, my_rows, :]

        if step == 1:
            mismatch, tied = tie_up()
        def send_dots():
            if step == 0:
                r.mismatch[...] = mismatch
                tied_row = fold(mismatch * tied)
            else:
                apart = r.mismatch[...] - alpha0 * mismatch
                tied_row = fold(apart * mix(coup, apart))
            wait(r.dot_z.at[step, pl.ds(0, nz - 1)], r.dz_rsem.at[step])
            r.dot_c[step, c] = jnp.sum(r.dot_z[step], axis=0) + jnp.where(row4 == 1, tied_row, 0.0)
            my_dots = r.dot_c.at[step, c]
            to_cohort(my_dots, my_dots, r.dc_ssem.at[step], r.dc_rsem.at[step])

        if step == 1:
            send_dots()

        tie = scatter((reach * prow, prow), tied, r.hot_g[...], r.key_g[...])
        local_a = local_a + slots_of(tie[0:prow, :] + tie[prow : 2 * prow, :])
        wait(r.back_recv.at[step, pl.ds(0, nz - 1)], r.bk_rsem.at[step])
        image_a = local_a + slots_of(jnp.sum(r.back_recv[step], axis=0))
        if step == 0:
            y_a = precond_a(image_a)
            for i in range(0, prow, 8):
                lo = i // TRAITS
                at = reach * prow + i
                r.field[1, at : at + 8, :] = jnp.concatenate(
                    [y_a[:, lo * HI : (lo + 1) * HI], y_a[:, (lo + 1) * HI : (lo + 2) * HI]], axis=0
                )
            mine = r.field.at[1, my_rows, :]
            to_snp(
                lambda k: mine, lambda k: r.field.at[1, pl.ds((reach - k) % nz * prow, prow), :],
                r.fl_ssem, lambda k: r.fl_rsem.at[0 if (reach - k) % nz < nears else 1], order,
            )
            r.y_own[...] = y_a
            r.image_a[...] = image_a
            send_own(1, r.y_own)
            send_dots()
        else:
            r.w_own[...] = image_a
            landing = r.w_a.at[:, my_slots]
            to_snp(lambda k: r.w_own, lambda k: landing, r.ra_ssem, lambda k: r.ra_rsem, order)
            r.w_a[:, my_slots] = image_a

        @pl.when(is_owner)
        def _():
            wait(r.sum_s.at[step, pl.ds(0, nc - 1)], r.ss_rsem.at[step])

        image_s = local_s - jnp.sum(jnp.where(is_owner, r.sum_s[step], 0.0), axis=0)
        if step == 0:
            r.image_s[...] = image_s
            y_s = precond_s(image_s, own_at)

            @pl.when(is_owner)
            def _():
                r.z_s[1, :, own_at] = y_s
                mine = r.z_s.at[1, :, own_at]
                to_cohort(mine, mine, r.zs_ssem, r.zs_rsem)
        else:

            @pl.when(is_owner)
            def _():
                r.w_s[:, own_at] = image_s
                mine = r.w_s.at[:, own_at]
                to_cohort(mine, mine, r.rs_ssem, r.rs_rsem)

    wait(r.dot_c.at[1, pl.ds(0, nc - 1)], r.dc_rsem.at[1])
    dots = jnp.sum(r.dot_c[1], axis=0)
    gamma1, delta_z, cross = (total_of(dots[i : i + 1, :]) for i in range(3))
    beta = gamma1 / gamma0
    alpha1 = gamma1 / (delta_z + 2.0 * beta * cross + beta * beta * delta0)

    once = alpha0 + alpha1 * (1.0 + beta)
    twice = alpha1 * alpha0
    wait(r.q_a.at[:, pl.ds(0, slots - part)], r.qa_rsem)
    wait(r.w_a.at[:, pl.ds(0, slots - part)], r.ra_rsem)

    @pl.loop(0, lows // 2, unroll=4)
    def _(j):
        here = pl.ds(pl.multiple_of(j * 2 * HI, 2 * HI), 2 * HI)
        y = r.field[1, place_of(j), :]
        y = jnp.concatenate([y[0:TRAITS, :], y[TRAITS:8, :]], axis=1)
        r.out_sol_a[:, here] = once * r.z_a0[:, here] - twice * y
        r.out_ra[:, here] = r.res_a0[:, here] - once * r.q_a[:, here] + twice * r.w_a[:, here]

    for full, sem in ((r.q_s, r.qs_rsem), (r.w_s, r.rs_rsem)):

        @pl.when(is_owner)
        def _():
            wait(full.at[:, pl.ds(0, (owners - 1) * OWN)], sem)

        @pl.when(jnp.logical_not(is_owner))
        def _():
            wait(full, sem)

    @pl.loop(0, owners, unroll=5)
    def _(j):
        here = pl.ds(pl.multiple_of(j * OWN, OWN), OWN)
        r.out_sol_s[:, here] = once * r.z_s[0, :, here] - twice * r.z_s[1, :, here]
        r.out_rs[:, here] = r.rhs_s[:, here] - once * r.q_s[:, here] + twice * r.w_s[:, here]

    for l in range(SPAN):
        wait(r.idx_own, r.idx_ssem.at[l])
    for step in range(2):
        wait(r.up_recv.at[step], r.up_ssem.at[step])
        wait(r.own_recv.at[step], r.own_ssem.at[step])
        wait(r.mk.at[step, pl.ds(0, nz - 1)], r.mk_ssem.at[step])
        wait(r.dot_z.at[step, pl.ds(0, nz - 1)], r.dz_ssem.at[step])
        wait(r.dot_c.at[step, pl.ds(0, nc - 1)], r.dc_ssem.at[step])
        wait(r.back_recv.at[step, pl.ds(0, nz - 1)], r.bk_ssem.at[step])

        @pl.when(is_owner)
        def _():
            wait(r.part_s.at[step, :, pl.ds(0, (owners - 1) * OWN)], r.ss_ssem.at[step])

        @pl.when(jnp.logical_not(is_owner))
        def _():
            wait(r.part_s.at[step], r.ss_ssem.at[step])

    @pl.when(is_owner)
    def _():
        for sem in (r.zs_ssem, r.qs_ssem, r.rs_ssem):
            wait(r.sum_s.at[0, pl.ds(0, nc - 1)], sem)

    wait(r.field.at[1, pl.ds(0, rows - prow), :], r.fl_ssem)
    wait(r.q_a.at[:, pl.ds(0, slots - part)], r.qa_ssem)
    wait(r.w_a.at[:, pl.ds(0, slots - part)], r.ra_ssem)


def place(*refs):
    half = len(refs) // 2
    for i in range(half):
        refs[half + i][...] = refs[i][...]


def body(nc, nz, rhs_a, rhs_s, weight, sire, dam, sizes, geno_idx, genotypes, pre_a, pre_s, *small):
    slots, snps, genos = rhs_a.shape[1], rhs_s.shape[1], geno_idx.shape[0]
    part = slots // nz
    rows = slots // HI * TRAITS
    chunk, chunks = snps, 1
    vmem, dma = pltpu.VMEM, pltpu.SemaphoreType.DMA
    inputs = dict(
        rhs_a=rhs_a, rhs_s=rhs_s, weight=weight[None], sire=sire[None], dam=dam[None], sizes=sizes[None],
        geno_idx=geno_idx[None], genotypes=genotypes, pre_a=pre_a, pre_s=pre_s,
        gen_inv=small[0], res_inv=small[1], coup=small[2], prior=small[3],
    )
    scratch = dict(
        rhs_a=vmem(rhs_a.shape, F32),
        rhs_s=vmem(rhs_s.shape, F32),
        weight=vmem((1, part), F32),
        sizes=vmem((1, nc), jnp.int32),
        geno_idx=vmem((1, genos), jnp.int32),
        pre_a=vmem(pre_a.shape, F32),
        pre_s=vmem(pre_s.shape, F32),
        gen_inv=vmem((TRAITS, TRAITS), F32),
        res_inv=vmem((TRAITS, TRAITS), F32),
        coup=vmem((TRAITS, TRAITS), F32),
        prior=vmem((TRAITS, TRAITS), F32),
        geno_f32=vmem((chunks, genos, chunk), F32),
        geno_hi=vmem((chunks, genos, chunk), BF16),
        geno_lo=vmem((chunks, genos, chunk), BF16),
        idx_own=vmem((2, 1, part), jnp.int32),
        idx_recv=vmem((SPAN, 2, 1, part), jnp.int32),
        hot=vmem((2 * SPAN, HI, part), BF16),
        key=vmem((2 * SPAN, 8, part), jnp.int32),
        hot_g=vmem((HI, genos), BF16),
        key_g=vmem((8, genos), jnp.int32),
        res_a0=vmem((TRAITS, slots), F32),
        z_a0=vmem((TRAITS, slots), F32),
        field=vmem((2, rows, HI), F32),
        field_bf=vmem((2 * rows, HI), BF16),
        partial=vmem((SPAN, 8, part), F32),
        z_s=vmem((2, TRAITS, snps), F32),
        acc_m=vmem((2 * TRAITS, genos), F32),
        mk=vmem((2, nz, TRAITS, genos), F32),
        part_s=vmem((2, TRAITS, snps), F32),
        sum_s=vmem((2, nc, TRAITS, OWN), F32),
        factor=vmem((SPAN, 1, part), F32),
        up_own=vmem((2, SPAN, TRAITS, part), F32),
        up_recv=vmem((2, 9, TRAITS, part), F32),
        own_recv=vmem((2, SPAN, TRAITS, part), F32),
        terms=vmem((SPAN, TRAITS, part), F32),
        dot_z=vmem((2, nz, 4, 128), F32),
        dot_c=vmem((2, nc, 4, 128), F32),
        acc_b=vmem((2 * rows, HI), F32),
        back=vmem((2, rows, HI), F32),
        back_recv=vmem((2, nz, rows // nz, HI), F32),
        image_a=vmem((TRAITS, part), F32),
        y_own=vmem((TRAITS, part), F32),
        w_own=vmem((TRAITS, part), F32),
        deviation=vmem((TRAITS, part), F32),
        mismatch=vmem((TRAITS, genos), F32),
        local_s=vmem((TRAITS, OWN), F32),
        image_s=vmem((TRAITS, OWN), F32),
        q_a=vmem((TRAITS, slots), F32),
        w_a=vmem((TRAITS, slots), F32),
        q_s=vmem((TRAITS, snps), F32),
        w_s=vmem((TRAITS, snps), F32),
        load_sem=dma((13 + chunks,)),
    )
    for name, shape in dict(
        idx=(SPAN,), up=(2,), own=(2,), mk=(2,), ss=(2,), dz=(2,), dc=(2,), bk=(2,), zs=(), rs=(), qs=(), qa=(), ra=(),
    ).items():
        scratch[name + "_ssem"] = dma(shape)
        scratch[name + "_rsem"] = dma(shape)
    scratch |= dict(fl_ssem=dma(()), fl_rsem=dma((2,)))
    names = ["in_" + name for name in inputs]
    names += ["out_sol_a", "out_sol_s", "out_ra", "out_rs"] + list(scratch)
    outs = [jax.ShapeDtypeStruct(x.shape, F32) for x in (rhs_a, rhs_s, rhs_a, rhs_s)]
    limit = 56 * 1024 * 1024
    results = pl.pallas_call(
        functools.partial(kernel, nc, nz, names),
        out_shape=outs,
        in_specs=[pl.BlockSpec(memory_space=pl.ANY)] * len(inputs),
        out_specs=[pl.BlockSpec(memory_space=pltpu.VMEM)] * 4,
        scratch_shapes=list(scratch.values()),
        compiler_params=pltpu.CompilerParams(collective_id=0, has_side_effects=True, vmem_limit_bytes=limit),
        cost_estimate=pl.CostEstimate(flops=4 * 10**9, bytes_accessed=10**7, transcendentals=0),
    )(*inputs.values())
    return pl.pallas_call(
        place,
        out_shape=outs,
        in_specs=[pl.BlockSpec(memory_space=pltpu.VMEM)] * 4,
        out_specs=[pl.BlockSpec(memory_space=pltpu.VMEM)] * 4,
    )(*results)


def solution(mesh):
    nc, nz = mesh.shape["cohort"], mesh.shape["snp"]
    in_specs = (
        P(None, "cohort"),
        P(None, "snp"),
        P("cohort"),
        P("cohort"),
        P("cohort"),
        P(),
        P("cohort"),
        P("cohort", "snp"),
        P(None, None, "cohort"),
        P(None, None, "snp"),
        P(),
        P(),
        P(),
        P(),
    )
    out_specs = (P(None, "cohort"), P(None, "snp"), P(None, "cohort"), P(None, "snp"))
    return jax.shard_map(
        functools.partial(body, nc, nz), mesh=mesh, in_specs=in_specs, out_specs=out_specs, check_vma=False
    )
```

```python
import functools
import types

import jax
import jax.numpy as jnp
from jax import lax
from jax.experimental import pallas as pl
from jax.experimental.pallas import tpu as pltpu
from jax.sharding import PartitionSpec as P

SPAN = 3
TRAITS = 4
HI = 256
OWN = 256
F32 = jnp.float32
BF16 = jnp.bfloat16
MESH = pl.DeviceIdType.MESH


def split(x):
    high = x.astype(BF16)
    return high, (x - high.astype(F32)).astype(BF16)


def stacked_split(x):
    high, low = split(x)
    return jnp.concatenate([high.astype(F32), low.astype(F32)], axis=0).astype(BF16)


def mix(matrix, field):
    total = matrix[:, 0:1] * field[0:1, :]
    for u in range(1, TRAITS):
        total = total + matrix[:, u : u + 1] * field[u : u + 1, :]
    return total


def fold(x):
    total = x[:, 0:128]
    for i in range(1, x.shape[1] // 128):
        total = total + x[:, i * 128 : (i + 1) * 128]
    return jnp.sum(total, axis=0, keepdims=True)


def total_of(row):
    return jnp.sum(row, axis=1, keepdims=True)


def z_plan(nz):
    order = sorted(range(1, nz), key=lambda k: -min(k, nz - k))
    return order, nz // 4


def kernel(nc, nz, names, *refs):
    r = types.SimpleNamespace(**dict(zip(names, refs)))
    c = lax.axis_index("cohort")
    z = lax.axis_index("snp")
    slots = r.rhs_a.shape[1]
    part = slots // nz
    lows = slots // HI
    rows = lows * TRAITS
    prow = rows // nz
    snps = r.rhs_s.shape[1]
    owners = snps // OWN
    chunk = r.geno_f32.shape[2]
    chunks = snps // chunk
    own_block = lax.rem(c, owners)
    is_owner = c < owners
    own_at = pl.ds(pl.multiple_of(own_block * OWN, OWN), OWN)
    my_slots = pl.ds(pl.multiple_of(z * part, part), part)
    order, reach = z_plan(nz)
    my_rows = slice(reach * prow, (reach + 1) * prow)

    def cohort_at(k):
        return lax.rem(c + k + nc, nc)

    def send(src, dst, send_sem, recv_sem, device):
        pltpu.make_async_remote_copy(
            src_ref=src, dst_ref=dst, send_sem=send_sem, recv_sem=recv_sem,
            device_id=device, device_id_type=MESH,
        ).start()

    def wait(ref, sem):
        pltpu.make_async_copy(ref, ref, sem).wait()

    loads = []
    for src, dst in (
        (r.in_rhs_a, r.rhs_a),
        (r.in_pre_a, r.pre_a),
        (r.in_sizes, r.sizes),
        (r.in_geno_idx, r.geno_idx),
        (r.in_rhs_s, r.rhs_s),
        (r.in_pre_s, r.pre_s),
        (r.in_weight.at[:, my_slots], r.weight),
        (r.in_gen_inv, r.gen_inv),
        (r.in_res_inv, r.res_inv),
        (r.in_coup, r.coup),
        (r.in_prior, r.prior),
    ):
        loads.append(pltpu.make_async_copy(src, dst, r.load_sem.at[len(loads)]))
    for j in range(chunks):
        loads.append(
            pltpu.make_async_copy(
                r.in_genotypes.at[:, j * chunk : (j + 1) * chunk], r.geno_f32.at[j], r.load_sem.at[len(loads)]
            )
        )
    for load in loads:
        load.start()

    barrier = pltpu.get_barrier_semaphore()

    @pl.loop(1, nz)
    def _(k):
        pl.semaphore_signal(barrier, inc=1, device_id=(c, lax.rem(z + k, nz)), device_id_type=MESH)

    @pl.loop(1, nc)
    def _(k):
        pl.semaphore_signal(barrier, inc=1, device_id=(cohort_at(k), z), device_id_type=MESH)

    pl.semaphore_wait(barrier, nz - 1 + nc - 1)

    for l in range(SPAN):
        for k, src in enumerate((r.in_sire, r.in_dam)):
            send(
                src.at[:, my_slots], r.idx_recv.at[l, k], r.idx_ssem.at[l], r.idx_rsem.at[l],
                (cohort_at(-(l + 1)), z),
            )

    def to_snp(src_of, dst_of, send_sem, recv_sem_of, ks):
        for k in ks:
            send(src_of(k), dst_of(k), send_sem, recv_sem_of(k), (c, lax.rem(z + k, nz)))

    def around(act):
        ny = min(4, nc // 2)
        nx = nc // (2 * ny)
        x, y, core = c // (2 * ny), c // 2 % ny, c % 2
        xs = [lax.rem(x + (i + nx // 2) % nx, nx) * (2 * ny) for i in range(nx)]
        ys = [lax.rem(y + (i + ny // 2) % ny, ny) * 2 for i in range(ny)]
        cores = [core, 1 - core]
        for i in range(nx):
            for j in range(ny):
                for k in range(2):
                    if (i + nx // 2) % nx or (j + ny // 2) % ny or k:
                        act(xs[i] + ys[j] + cores[k])

    def to_cohort(src, dst, send_sem, recv_sem):
        around(lambda other: send(src, dst, send_sem, recv_sem, (other, z)))

    for load in loads[:3]:
        load.wait()

    cohort_row = lax.broadcasted_iota(jnp.int32, (1, nc), 1)
    live_count = total_of(jnp.where(cohort_row == c, r.sizes[...].astype(F32), 0.0))

    def place_of(j):
        at = lax.rem(j + lows // 2 - z * (prow // 8) + reach * (prow // 8), lows // 2)
        return pl.ds(pl.multiple_of(at * 8, 8), 8)

    @pl.loop(0, lows // 2, unroll=4)
    def _(j):
        here = pl.ds(pl.multiple_of(j * 2 * HI, 2 * HI), 2 * HI)
        slot = (lax.broadcasted_iota(jnp.int32, (1, 2 * HI), 1) + j * 2 * HI).astype(F32)
        res = jnp.where(slot < live_count, r.rhs_a[:, here], 0.0)
        r.res_a0[:, here] = res
        pre = r.pre_a[0, :, here] * res[0:1, :]
        for u in range(1, TRAITS):
            pre = pre + r.pre_a[u, :, here] * res[u : u + 1, :]
        r.z_a0[:, here] = pre
        r.field[0, place_of(j), :] = jnp.concatenate([pre[:, :HI], pre[:, HI:]], axis=0)

    def precond_s(res, at):
        pre = r.pre_s[0, :, at] * res[0:1, :]
        for u in range(1, TRAITS):
            pre = pre + r.pre_s[u, :, at] * res[u : u + 1, :]
        return pre

    def precond_a(res):
        pre = r.pre_a[0, :, my_slots] * res[0:1, :]
        for u in range(1, TRAITS):
            pre = pre + r.pre_a[u, :, my_slots] * res[u : u + 1, :]
        return pre

    def marker_product(step):
        r.acc_m[...] = jnp.zeros_like(r.acc_m)

        @pl.loop(0, chunks)
        def _(j):
            at = pl.ds(pl.multiple_of(j * chunk, chunk), chunk)
            if step == 0:
                z_s = precond_s(r.rhs_s[:, at], at)
                r.z_s[0, :, at] = z_s
                high, low = split(r.geno_f32[j])
                r.geno_hi[j] = high
                r.geno_lo[j] = low
            else:
                z_s = r.z_s[step, :, at]
                high, low = r.geno_hi[j], r.geno_lo[j]
            both = stacked_split(z_s)
            dims = (((1,), (1,)), ((), ()))
            r.acc_m[...] += lax.dot_general(
                both, high, dims, preferred_element_type=F32
            ) + lax.dot_general(both, low, dims, preferred_element_type=F32)

        r.mk[step, z] = r.acc_m[0:TRAITS, :] + r.acc_m[TRAITS : 2 * TRAITS, :]
        mine = r.mk.at[step, z]
        to_snp(lambda k: mine, lambda k: mine, r.mk_ssem.at[step], lambda k: r.mk_rsem.at[step], order)

    first_animal = c * slots

    def one_hot(index):
        local = index - first_animal
        high = jnp.bitwise_and(local, HI - 1)
        low = jnp.right_shift(local, 8)
        n = index.shape[1]
        hot = (lax.broadcasted_iota(jnp.int32, (HI, n), 0) == high).astype(F32).astype(BF16)
        here = jnp.logical_and(low >= 0, low < lows)
        around_low = jnp.bitwise_and(low + (reach - z) * (lows // nz), lows - 1)
        place = jnp.where(here, around_low, -8)
        return hot, place - jnp.right_shift(lax.broadcasted_iota(jnp.int32, (8, n), 0), 2)

    def load_field(step, which):
        first, count = which
        high, low = split(r.field[step, first : first + count, :])
        r.field_bf[2 * first : 2 * first + count, :] = high
        r.field_bf[2 * first + count : 2 * (first + count), :] = low

    def gather(which, hot, key):
        first, count = which
        picked = jnp.dot(
            r.field_bf[2 * first : 2 * (first + count), :], hot, preferred_element_type=F32
        )
        total = jnp.zeros((8, hot.shape[1]), F32)
        for g in range(count // 8):
            value = picked[g * 8 : g * 8 + 8, :] + picked[count + g * 8 : count + g * 8 + 8, :]
            total = total + jnp.where(key == 2 * (g + first // 8), value, 0.0)
        return total

    def gather_all(which, l):
        return gather(which, r.hot[2 * l], r.key[2 * l]) + gather(which, r.hot[2 * l + 1], r.key[2 * l + 1])

    def halves(total):
        return total[0:TRAITS, :] + total[TRAITS:8, :]

    def scatter(which, value, hot, key):
        first, count = which
        high, low = split(jnp.concatenate([value, value], axis=0))
        pieces = []
        for piece in (high.astype(F32), low.astype(F32)):
            for g in range(count // 8):
                pieces.append(jnp.where(key == 2 * (g + first // 8), piece, 0.0))
        spread = jnp.concatenate(pieces, axis=0).astype(BF16)
        return lax.dot_general(spread, hot, (((1,), (1,)), ((), ())), preferred_element_type=F32)

    def slots_of(block):
        return jnp.concatenate([block[i : i + TRAITS, :] for i in range(0, prow, TRAITS)], axis=1)

    readers = (((-2, 4), (-1, 3)), ((1, 0), (-1, 5)), ((2, 2), (1, 1)))

    def send_sums_up(step, l):
        def to(readers_l):
            for offset, place_there in readers_l:
                send(
                    r.up_own.at[step, l], r.up_recv.at[step, place_there],
                    r.up_ssem.at[step], r.up_rsem.at[step], (cohort_at(offset), z),
                )

        if isinstance(l, int):
            to(readers[l])
        else:
            for i in range(SPAN):
                pl.when(l == i)(functools.partial(to, readers[i]))

    def send_own(step, src):
        for l in reversed(range(SPAN)):
            send(
                src, r.own_recv.at[step, l], r.own_ssem.at[step], r.own_rsem.at[step], (cohort_at(-(l + 1)), z)
            )

    def factor_of(sire, dam):
        known = jnp.where(sire >= 0, 1.0, 0.0) + jnp.where(dam >= 0, 1.0, 0.0)
        return 4.0 / (4.0 - known)

    row4 = lax.broadcasted_iota(jnp.int32, (4, 128), 0)
    at_owner = jnp.where(is_owner, 1.0, 0.0)
    whole = (0, rows)

    send_own(0, r.z_a0.at[:, my_slots])
    for load in loads[3:]:
        load.wait()
    gen_inv, res_inv, coup, prior = (x[...] for x in (r.gen_inv, r.res_inv, r.coup, r.prior))

    for step in range(2):
        if step == 0:
            marker_product(0)
            load_field(0, whole)

            for l in reversed(range(SPAN)):
                wait(r.idx_recv.at[l], r.idx_rsem.at[l])
                for k in range(2):
                    hot, key = one_hot(r.idx_recv[l, k])
                    r.hot[2 * l + k] = hot
                    r.key[2 * l + k] = key
                r.up_own[0, l] = halves(gather_all(whole, l))
                send_sums_up(0, l)
                r.factor[l] = factor_of(r.idx_recv[l, 0], r.idx_recv[l, 1])

            hot, key = one_hot(r.geno_idx[...])
            r.hot_g[...] = hot
            r.key_g[...] = key
        else:
            wait(r.field.at[1, pl.ds(0, rows - prow), :], r.fl_rsem)
            load_field(1, whole)

            for l in reversed(range(SPAN)):
                total = gather_all(whole, l)
                r.up_own[1, l] = halves(total)
                send_sums_up(1, l)

            @pl.when(is_owner)
            def _():
                wait(r.z_s.at[1, :, pl.ds(0, (owners - 1) * OWN)], r.zs_rsem)

            @pl.when(jnp.logical_not(is_owner))
            def _():
                wait(r.z_s.at[1], r.zs_rsem)

            marker_product(1)

            to_snp(
                lambda k: r.image_a, lambda k: r.q_a.at[:, my_slots], r.qa_ssem, lambda k: r.qa_rsem, order
            )
            r.q_a[:, my_slots] = r.image_a[...]

            @pl.when(is_owner)
            def _():
                r.q_s[:, own_at] = r.image_s[...]
                mine = r.q_s.at[:, own_at]
                to_cohort(mine, mine, r.qs_ssem, r.qs_rsem)

        dir_g = halves(gather(whole, r.hot_g[...], r.key_g[...]))

        def tie_up():
            wait(r.mk.at[step, pl.ds(0, nz - 1)], r.mk_rsem.at[step])
            mismatch = dir_g - jnp.sum(r.mk[step], axis=0)
            tied = mix(coup, mismatch)

            both = stacked_split(tied)

            @pl.loop(0, chunks)
            def _(j):
                at = pl.ds(pl.multiple_of(j * chunk, chunk), chunk)
                sums = jnp.dot(both, r.geno_hi[j], preferred_element_type=F32) + jnp.dot(
                    both, r.geno_lo[j], preferred_element_type=F32
                )
                r.part_s[step, :, at] = sums[0:TRAITS, :] + sums[TRAITS : 2 * TRAITS, :]

            r.sum_s[step, c] = r.part_s[step, :, own_at]

            def send_sums(other):
                @pl.when(other < owners)
                def _():
                    send(
                        r.part_s.at[step, :, pl.ds(pl.multiple_of(other * OWN, OWN), OWN)],
                        r.sum_s.at[step, c], r.ss_ssem.at[step], r.ss_rsem.at[step], (other, z),
                    )

            return mismatch, tied, send_sums

        if step == 0:
            mismatch, tied, send_sums = tie_up()

        wait(r.own_recv.at[step], r.own_rsem.at[step])
        wait(r.up_recv.at[step], r.up_rsem.at[step])
        others = ((0, 2), (1, 3), (5, 4))
        for l in range(SPAN):
            parents = r.up_own[step, l] + r.up_recv[step, others[l][0]] + r.up_recv[step, others[l][1]]
            apart_l = r.own_recv[step, l] - 0.5 * parents
            mixed_l = mix(gen_inv, r.factor[l] * apart_l)
            r.terms[l] = -0.5 * mixed_l
            if l == 0:
                deviation, mixed = apart_l, mixed_l
                r.mixed[step] = mixed
                send(
                    r.mixed.at[step], r.down_recv.at[step],
                    r.down_ssem.at[step], r.down_rsem.at[step], (cohort_at(1), z),
                )

        own = r.z_a0[:, my_slots] if step == 0 else r.y_own[...]
        local_a = r.weight[...] * mix(res_inv, own)
        own_s = r.z_s[step, :, own_at]
        local_s = mix(prior, own_s)
        if step == 0:
            r.local_s[...] = local_s
            r.deviation[...] = deviation
            curve = fold(own * local_a + deviation * mixed) + at_owner * fold(own_s * local_s)
            gamma_row = fold(own * r.res_a0[:, my_slots]) + at_owner * fold(own_s * r.rhs_s[:, own_at])
            cross_row = jnp.zeros((1, 128), F32)
        else:
            wait(r.dot_c.at[0, pl.ds(0, nc - 1)], r.dc_rsem.at[0])
            dots = jnp.sum(r.dot_c[0], axis=0)
            gamma0, delta0 = total_of(dots[0:1, :]), total_of(dots[1:2, :])
            alpha0 = gamma0 / delta0
            z_own = r.z_a0[:, my_slots] - alpha0 * own
            res_a1 = r.res_a0[:, my_slots] - alpha0 * r.image_a[...]
            zs_own = r.z_s[0, :, own_at] - alpha0 * own_s
            res_s1 = r.rhs_s[:, own_at] - alpha0 * r.image_s[...]
            gamma_row = fold(z_own * res_a1) + at_owner * fold(zs_own * res_s1)
            cross_row = fold(z_own * r.image_a[...]) + at_owner * fold(zs_own * r.image_s[...])
            deviation = r.deviation[...] - alpha0 * deviation
            z_mixed = mix(gen_inv, r.factor[0] * deviation)
            record = r.weight[...] * mix(res_inv, z_own)
            curve = fold(z_own * record + deviation * z_mixed) + at_owner * fold(
                zs_own * (r.local_s[...] - alpha0 * local_s)
            )
        r.dot_z[step, z] = jnp.where(
            row4 == 0, gamma_row, jnp.where(row4 == 1, curve, jnp.where(row4 == 2, cross_row, 0.0))
        )
        my_dots = r.dot_z.at[step, z]
        to_snp(lambda k: my_dots, lambda k: my_dots, r.dz_ssem.at[step], lambda k: r.dz_rsem.at[step], order)

        r.acc_b[...] = jnp.zeros_like(r.acc_b)

        @pl.loop(0, SPAN)
        def _(l):
            r.acc_b[...] += scatter(whole, r.terms[l], r.hot[2 * l], r.key[2 * l]) + scatter(
                whole, r.terms[l], r.hot[2 * l + 1], r.key[2 * l + 1]
            )

        r.back[step] = r.acc_b[0:rows, :] + r.acc_b[rows : 2 * rows, :]
        to_snp(
            lambda k: r.back.at[step, pl.ds((k + reach) % nz * prow, prow), :],
            lambda k: r.back_recv.at[step, k], r.bk_ssem.at[step], lambda k: r.bk_rsem.at[step], order,
        )
        r.back_recv[step, 0] = r.back[step, my_rows, :]

        if step == 1:
            mismatch, tied, send_sums = tie_up()
        around(send_sums)
        def send_dots():
            if step == 0:
                r.mismatch[...] = mismatch
                tied_row = fold(mismatch * tied)
            else:
                apart = r.mismatch[...] - alpha0 * mismatch
                tied_row = fold(apart * mix(coup, apart))
            wait(r.dot_z.at[step, pl.ds(0, nz - 1)], r.dz_rsem.at[step])
            r.dot_c[step, c] = jnp.sum(r.dot_z[step], axis=0) + jnp.where(row4 == 1, tied_row, 0.0)
            my_dots = r.dot_c.at[step, c]
            to_cohort(my_dots, my_dots, r.dc_ssem.at[step], r.dc_rsem.at[step])

        if step == 1:
            send_dots()

        tie = scatter((reach * prow, prow), tied, r.hot_g[...], r.key_g[...])
        local_a = local_a + slots_of(tie[0:prow, :] + tie[prow : 2 * prow, :])
        wait(r.down_recv.at[step], r.down_rsem.at[step])
        local_a = local_a + r.down_recv[step]
        wait(r.back_recv.at[step, pl.ds(0, nz - 1)], r.bk_rsem.at[step])
        image_a = local_a + slots_of(jnp.sum(r.back_recv[step], axis=0))
        if step == 0:
            y_a = precond_a(image_a)
            for i in range(0, prow, 8):
                lo = i // TRAITS
                at = reach * prow + i
                r.field[1, at : at + 8, :] = jnp.concatenate(
                    [y_a[:, lo * HI : (lo + 1) * HI], y_a[:, (lo + 1) * HI : (lo + 2) * HI]], axis=0
                )
            mine = r.field.at[1, my_rows, :]
            to_snp(
                lambda k: mine, lambda k: r.field.at[1, pl.ds((reach - k) % nz * prow, prow), :],
                r.fl_ssem, lambda k: r.fl_rsem, order,
            )
            r.y_own[...] = y_a
            r.image_a[...] = image_a
            send_own(1, r.y_own)
            send_dots()
        else:
            r.w_own[...] = image_a
            landing = r.out_w_a.at[:, my_slots]
            to_snp(lambda k: r.w_own, lambda k: landing, r.ra_ssem, lambda k: r.ra_rsem, order)
            pltpu.make_async_copy(r.w_own, landing, r.out_sem.at[5]).start()

        @pl.when(is_owner)
        def _():
            wait(r.sum_s.at[step, pl.ds(0, nc - 1)], r.ss_rsem.at[step])

        image_s = local_s - jnp.sum(jnp.where(is_owner, r.sum_s[step], 0.0), axis=0)
        if step == 0:
            r.image_s[...] = image_s
            y_s = precond_s(image_s, own_at)

            @pl.when(is_owner)
            def _():
                r.z_s[1, :, own_at] = y_s
                mine = r.z_s.at[1, :, own_at]
                to_cohort(mine, mine, r.zs_ssem, r.zs_rsem)
        else:

            @pl.when(is_owner)
            def _():
                r.ws_own[...] = image_s
                landing = r.out_w_s.at[:, own_at]
                to_cohort(r.ws_own, landing, r.rs_ssem, r.rs_rsem)
                pltpu.make_async_copy(r.ws_own, landing, r.out_sem.at[6]).start()

    wait(r.dot_c.at[1, pl.ds(0, nc - 1)], r.dc_rsem.at[1])
    dots = jnp.sum(r.dot_c[1], axis=0)
    gamma1, delta_z, cross = (total_of(dots[i : i + 1, :]) for i in range(3))
    beta = gamma1 / gamma0
    alpha1 = gamma1 / (delta_z + 2.0 * beta * cross + beta * beta * delta0)

    once = alpha0 + alpha1 * (1.0 + beta)
    twice = alpha1 * alpha0
    wait(r.q_a.at[:, pl.ds(0, slots - part)], r.qa_rsem)

    @pl.loop(0, lows // 2, unroll=4)
    def _(j):
        here = pl.ds(pl.multiple_of(j * 2 * HI, 2 * HI), 2 * HI)
        y = r.field[1, place_of(j), :]
        y = jnp.concatenate([y[0:TRAITS, :], y[TRAITS:8, :]], axis=1)
        r.sol_a[:, here] = once * r.z_a0[:, here] - twice * y
        r.left_a[:, here] = r.res_a0[:, here] - once * r.q_a[:, here]

    def arrived(full, sem):
        @pl.when(is_owner)
        def _():
            wait(full.at[:, pl.ds(0, (owners - 1) * OWN)], sem)

        @pl.when(jnp.logical_not(is_owner))
        def _():
            wait(full, sem)

    arrived(r.q_s, r.qs_rsem)

    @pl.loop(0, owners, unroll=5)
    def _(j):
        here = pl.ds(pl.multiple_of(j * OWN, OWN), OWN)
        r.sol_s[:, here] = once * r.z_s[0, :, here] - twice * r.z_s[1, :, here]
        r.left_s[:, here] = r.rhs_s[:, here] - once * r.q_s[:, here]

    r.scale[...] = jnp.broadcast_to(twice, r.scale.shape)
    stores = [
        pltpu.make_async_copy(src, dst, r.out_sem.at[i])
        for i, (src, dst) in enumerate(
            (
                (r.sol_a, r.out_sol_a), (r.sol_s, r.out_sol_s), (r.left_a, r.out_left_a),
                (r.left_s, r.out_left_s), (r.scale, r.out_scale),
            )
        )
    ]
    for store in stores:
        store.start()

    for l in range(SPAN):
        wait(r.idx_recv.at[l], r.idx_ssem.at[l])
    for step in range(2):
        wait(r.up_recv.at[step], r.up_ssem.at[step])
        wait(r.own_recv.at[step], r.own_ssem.at[step])
        wait(r.mixed.at[step], r.down_ssem.at[step])
        wait(r.mk.at[step, pl.ds(0, nz - 1)], r.mk_ssem.at[step])
        wait(r.dot_z.at[step, pl.ds(0, nz - 1)], r.dz_ssem.at[step])
        wait(r.dot_c.at[step, pl.ds(0, nc - 1)], r.dc_ssem.at[step])
        wait(r.back_recv.at[step, pl.ds(0, nz - 1)], r.bk_ssem.at[step])

        @pl.when(is_owner)
        def _():
            wait(r.part_s.at[step, :, pl.ds(0, (owners - 1) * OWN)], r.ss_ssem.at[step])

        @pl.when(jnp.logical_not(is_owner))
        def _():
            wait(r.part_s.at[step], r.ss_ssem.at[step])

    @pl.when(is_owner)
    def _():
        for sem in (r.zs_ssem, r.qs_ssem, r.rs_ssem):
            wait(r.sum_s.at[0, pl.ds(0, nc - 1)], sem)

    wait(r.field.at[1, pl.ds(0, rows - prow), :], r.fl_ssem)
    wait(r.q_a.at[:, pl.ds(0, slots - part)], r.qa_ssem)
    wait(r.q_a.at[:, pl.ds(0, slots - part)], r.ra_ssem)
    for store in stores:
        store.wait()
    pltpu.make_async_copy(r.w_own, r.out_w_a.at[:, my_slots], r.out_sem.at[5]).wait()
    wait(r.sol_a.at[:, pl.ds(0, slots - part)], r.ra_rsem)

    @pl.when(is_owner)
    def _():
        pltpu.make_async_copy(r.ws_own, r.out_w_s.at[:, own_at], r.out_sem.at[6]).wait()

    arrived(r.sol_s, r.rs_rsem)


def place(sol_a, sol_s, left_a, left_s, w_a, w_s, scale, out_sol_a, out_sol_s, out_ra, out_rs):
    twice = scale[0:1, 0:1]
    out_sol_a[...] = sol_a[...]
    out_sol_s[...] = sol_s[...]
    out_ra[...] = left_a[...] + twice * w_a[...]
    out_rs[...] = left_s[...] + twice * w_s[...]


def body(nc, nz, rhs_a, rhs_s, weight, sire, dam, sizes, geno_idx, genotypes, pre_a, pre_s, *small):
    slots, snps, genos = rhs_a.shape[1], rhs_s.shape[1], geno_idx.shape[0]
    part = slots // nz
    rows = slots // HI * TRAITS
    chunk, chunks = snps, 1
    vmem, dma = pltpu.VMEM, pltpu.SemaphoreType.DMA
    inputs = dict(
        rhs_a=rhs_a, rhs_s=rhs_s, weight=weight[None], sire=sire[None], dam=dam[None], sizes=sizes[None],
        geno_idx=geno_idx[None], genotypes=genotypes, pre_a=pre_a, pre_s=pre_s,
        gen_inv=small[0], res_inv=small[1], coup=small[2], prior=small[3],
    )
    scratch = dict(
        rhs_a=vmem(rhs_a.shape, F32),
        rhs_s=vmem(rhs_s.shape, F32),
        weight=vmem((1, part), F32),
        sizes=vmem((1, nc), jnp.int32),
        geno_idx=vmem((1, genos), jnp.int32),
        pre_a=vmem(pre_a.shape, F32),
        pre_s=vmem(pre_s.shape, F32),
        gen_inv=vmem((TRAITS, TRAITS), F32),
        res_inv=vmem((TRAITS, TRAITS), F32),
        coup=vmem((TRAITS, TRAITS), F32),
        prior=vmem((TRAITS, TRAITS), F32),
        geno_f32=vmem((chunks, genos, chunk), F32),
        geno_hi=vmem((chunks, genos, chunk), BF16),
        geno_lo=vmem((chunks, genos, chunk), BF16),
        idx_recv=vmem((SPAN, 2, 1, part), jnp.int32),
        hot=vmem((2 * SPAN, HI, part), BF16),
        key=vmem((2 * SPAN, 8, part), jnp.int32),
        hot_g=vmem((HI, genos), BF16),
        key_g=vmem((8, genos), jnp.int32),
        res_a0=vmem((TRAITS, slots), F32),
        z_a0=vmem((TRAITS, slots), F32),
        field=vmem((2, rows, HI), F32),
        field_bf=vmem((2 * rows, HI), BF16),
        z_s=vmem((2, TRAITS, snps), F32),
        acc_m=vmem((2 * TRAITS, genos), F32),
        mk=vmem((2, nz, TRAITS, genos), F32),
        part_s=vmem((2, TRAITS, snps), F32),
        sum_s=vmem((2, nc, TRAITS, OWN), F32),
        factor=vmem((SPAN, 1, part), F32),
        up_own=vmem((2, SPAN, TRAITS, part), F32),
        up_recv=vmem((2, 6, TRAITS, part), F32),
        mixed=vmem((2, TRAITS, part), F32),
        down_recv=vmem((2, TRAITS, part), F32),
        own_recv=vmem((2, SPAN, TRAITS, part), F32),
        terms=vmem((SPAN, TRAITS, part), F32),
        dot_z=vmem((2, nz, 4, 128), F32),
        dot_c=vmem((2, nc, 4, 128), F32),
        acc_b=vmem((2 * rows, HI), F32),
        back=vmem((2, rows, HI), F32),
        back_recv=vmem((2, nz, rows // nz, HI), F32),
        image_a=vmem((TRAITS, part), F32),
        y_own=vmem((TRAITS, part), F32),
        w_own=vmem((TRAITS, part), F32),
        deviation=vmem((TRAITS, part), F32),
        mismatch=vmem((TRAITS, genos), F32),
        local_s=vmem((TRAITS, OWN), F32),
        image_s=vmem((TRAITS, OWN), F32),
        q_a=vmem((TRAITS, slots), F32),
        sol_a=vmem((TRAITS, slots), F32),
        left_a=vmem((TRAITS, slots), F32),
        q_s=vmem((TRAITS, snps), F32),
        ws_own=vmem((TRAITS, OWN), F32),
        sol_s=vmem((TRAITS, snps), F32),
        left_s=vmem((TRAITS, snps), F32),
        scale=vmem((8, 128), F32),
        out_sem=dma((7,)),
        load_sem=dma((11 + chunks,)),
    )
    for name, shape in dict(
        idx=(SPAN,), up=(2,), own=(2,), down=(2,), mk=(2,), ss=(2,), dz=(2,), dc=(2,), bk=(2,), zs=(), rs=(), qs=(), qa=(), fl=(), ra=(),
    ).items():
        scratch[name + "_ssem"] = dma(shape)
        scratch[name + "_rsem"] = dma(shape)
    names = ["in_" + name for name in inputs]
    names += ["out_sol_a", "out_sol_s", "out_left_a", "out_left_s", "out_w_a", "out_w_s", "out_scale"] + list(scratch)
    outs = [jax.ShapeDtypeStruct(x.shape, F32) for x in (rhs_a, rhs_s, rhs_a, rhs_s)]
    limit = 56 * 1024 * 1024
    results = pl.pallas_call(
        functools.partial(kernel, nc, nz, names),
        out_shape=outs + outs[:2] + [jax.ShapeDtypeStruct((8, 128), F32)],
        in_specs=[pl.BlockSpec(memory_space=pl.ANY)] * len(inputs),
        out_specs=[pl.BlockSpec(memory_space=pl.ANY)] * 7,
        scratch_shapes=list(scratch.values()),
        compiler_params=pltpu.CompilerParams(collective_id=0, has_side_effects=True, vmem_limit_bytes=limit),
        cost_estimate=pl.CostEstimate(flops=4 * 10**9, bytes_accessed=10**7, transcendentals=0),
    )(*inputs.values())
    return pl.pallas_call(
        place,
        out_shape=outs,
        in_specs=[pl.BlockSpec(memory_space=pltpu.VMEM)] * 7,
        out_specs=[pl.BlockSpec(memory_space=pltpu.VMEM)] * 4,
    )(*results)


def solution(mesh):
    nc, nz = mesh.shape["cohort"], mesh.shape["snp"]
    in_specs = (
        P(None, "cohort"),
        P(None, "snp"),
        P("cohort"),
        P("cohort"),
        P("cohort"),
        P(),
        P("cohort"),
        P("cohort", "snp"),
        P(None, None, "cohort"),
        P(None, None, "snp"),
        P(),
        P(),
        P(),
        P(),
    )
    out_specs = (P(None, "cohort"), P(None, "snp"), P(None, "cohort"), P(None, "snp"))
    return jax.shard_map(
        functools.partial(body, nc, nz), mesh=mesh, in_specs=in_specs, out_specs=out_specs, check_vma=False
    )
```

```python
import functools
import types

import jax
import jax.numpy as jnp
from jax import lax
from jax.experimental import pallas as pl
from jax.experimental.pallas import tpu as pltpu
from jax.sharding import PartitionSpec as P

SPAN = 3
TRAITS = 4
HI = 256
OWN = 256
F32 = jnp.float32
BF16 = jnp.bfloat16
MESH = pl.DeviceIdType.MESH


def split(x):
    high = x.astype(BF16)
    return high, (x - high.astype(F32)).astype(BF16)


def stacked_split(x):
    high, low = split(x)
    return jnp.concatenate([high.astype(F32), low.astype(F32)], axis=0).astype(BF16)


def mix(matrix, field):
    total = matrix[:, 0:1] * field[0:1, :]
    for u in range(1, TRAITS):
        total = total + matrix[:, u : u + 1] * field[u : u + 1, :]
    return total


def fold(x):
    total = x[:, 0:128]
    for i in range(1, x.shape[1] // 128):
        total = total + x[:, i * 128 : (i + 1) * 128]
    return jnp.sum(total, axis=0, keepdims=True)


def total_of(row):
    return jnp.sum(row, axis=1, keepdims=True)


def z_plan(nz):
    order = sorted(range(1, nz), key=lambda k: -min(k, nz - k))
    return order, nz // 4


def kernel(nc, nz, names, *refs):
    r = types.SimpleNamespace(**dict(zip(names, refs)))
    c = lax.axis_index("cohort")
    z = lax.axis_index("snp")
    slots = r.rhs_a.shape[1]
    part = slots // nz
    lows = slots // HI
    rows = lows * TRAITS
    prow = rows // nz
    snps = r.rhs_s.shape[1]
    owners = snps // OWN
    chunk = r.geno_f32.shape[2]
    chunks = snps // chunk
    own_block = lax.rem(c, owners)
    is_owner = c < owners
    own_at = pl.ds(pl.multiple_of(own_block * OWN, OWN), OWN)
    my_slots = pl.ds(pl.multiple_of(z * part, part), part)
    order, reach = z_plan(nz)
    my_rows = slice(reach * prow, (reach + 1) * prow)

    def cohort_at(k):
        return lax.rem(c + k + nc, nc)

    def send(src, dst, send_sem, recv_sem, device):
        pltpu.make_async_remote_copy(
            src_ref=src, dst_ref=dst, send_sem=send_sem, recv_sem=recv_sem,
            device_id=device, device_id_type=MESH,
        ).start()

    def wait(ref, sem):
        pltpu.make_async_copy(ref, ref, sem).wait()

    loads = []
    for src, dst in (
        (r.in_rhs_a, r.rhs_a),
        (r.in_pre_a, r.pre_a),
        (r.in_sizes, r.sizes),
        (r.in_geno_idx, r.geno_idx),
        (r.in_rhs_s, r.rhs_s),
        (r.in_pre_s, r.pre_s),
        (r.in_weight.at[:, my_slots], r.weight),
        (r.in_gen_inv, r.gen_inv),
        (r.in_res_inv, r.res_inv),
        (r.in_coup, r.coup),
        (r.in_prior, r.prior),
    ):
        loads.append(pltpu.make_async_copy(src, dst, r.load_sem.at[len(loads)]))
    for j in range(chunks):
        loads.append(
            pltpu.make_async_copy(
                r.in_genotypes.at[:, j * chunk : (j + 1) * chunk], r.geno_f32.at[j], r.load_sem.at[len(loads)]
            )
        )
    for load in loads:
        load.start()

    barrier = pltpu.get_barrier_semaphore()

    @pl.loop(1, nz)
    def _(k):
        pl.semaphore_signal(barrier, inc=1, device_id=(c, lax.rem(z + k, nz)), device_id_type=MESH)

    @pl.loop(1, nc)
    def _(k):
        pl.semaphore_signal(barrier, inc=1, device_id=(cohort_at(k), z), device_id_type=MESH)

    pl.semaphore_wait(barrier, nz - 1 + nc - 1)

    for l in range(SPAN):
        for k, src in enumerate((r.in_sire, r.in_dam)):
            send(
                src.at[:, my_slots], r.idx_recv.at[l, k], r.idx_ssem.at[l], r.idx_rsem.at[l],
                (cohort_at(-(l + 1)), z),
            )

    def to_snp(src_of, dst_of, send_sem, recv_sem_of, ks):
        for k in ks:
            send(src_of(k), dst_of(k), send_sem, recv_sem_of(k), (c, lax.rem(z + k, nz)))

    def around(act):
        ny = min(4, nc // 2)
        nx = nc // (2 * ny)
        x, y, core = c // (2 * ny), c // 2 % ny, c % 2
        ys = [lax.rem(y + (j + ny // 2) % ny, ny) * 2 for j in range(ny)]

        @pl.loop(0, nx)
        def _(i):
            to_x = lax.rem(x + i + nx // 2, nx) * (2 * ny)
            for j in range(ny):
                for to_core in (core, 1 - core):
                    other = to_x + ys[j] + to_core
                    if to_core is core and (j + ny // 2) % ny == 0:
                        pl.when(other != c)(functools.partial(act, other))
                    else:
                        act(other)

    def to_cohort(src, dst, send_sem, recv_sem):
        around(lambda other: send(src, dst, send_sem, recv_sem, (other, z)))

    for load in loads[:3]:
        load.wait()

    cohort_row = lax.broadcasted_iota(jnp.int32, (1, nc), 1)
    live_count = total_of(jnp.where(cohort_row == c, r.sizes[...].astype(F32), 0.0))

    def place_of(j):
        at = lax.rem(j + lows // 2 - z * (prow // 8) + reach * (prow // 8), lows // 2)
        return pl.ds(pl.multiple_of(at * 8, 8), 8)

    @pl.loop(0, lows // 2, unroll=4)
    def _(j):
        here = pl.ds(pl.multiple_of(j * 2 * HI, 2 * HI), 2 * HI)
        slot = (lax.broadcasted_iota(jnp.int32, (1, 2 * HI), 1) + j * 2 * HI).astype(F32)
        res = jnp.where(slot < live_count, r.rhs_a[:, here], 0.0)
        r.res_a0[:, here] = res
        pre = r.pre_a[0, :, here] * res[0:1, :]
        for u in range(1, TRAITS):
            pre = pre + r.pre_a[u, :, here] * res[u : u + 1, :]
        r.z_a0[:, here] = pre
        r.field[0, place_of(j), :] = jnp.concatenate([pre[:, :HI], pre[:, HI:]], axis=0)

    def precond_s(res, at):
        pre = r.pre_s[0, :, at] * res[0:1, :]
        for u in range(1, TRAITS):
            pre = pre + r.pre_s[u, :, at] * res[u : u + 1, :]
        return pre

    def precond_a(res):
        pre = r.pre_a[0, :, my_slots] * res[0:1, :]
        for u in range(1, TRAITS):
            pre = pre + r.pre_a[u, :, my_slots] * res[u : u + 1, :]
        return pre

    def marker_product(step):
        r.acc_m[...] = jnp.zeros_like(r.acc_m)

        @pl.loop(0, chunks)
        def _(j):
            at = pl.ds(pl.multiple_of(j * chunk, chunk), chunk)
            if step == 0:
                z_s = precond_s(r.rhs_s[:, at], at)
                r.z_s[0, :, at] = z_s
                high, low = split(r.geno_f32[j])
                r.geno_hi[j] = high
                r.geno_lo[j] = low
            else:
                z_s = r.z_s[step, :, at]
                high, low = r.geno_hi[j], r.geno_lo[j]
            both = stacked_split(z_s)
            dims = (((1,), (1,)), ((), ()))
            r.acc_m[...] += lax.dot_general(
                both, high, dims, preferred_element_type=F32
            ) + lax.dot_general(both, low, dims, preferred_element_type=F32)

        r.mk[step, z] = r.acc_m[0:TRAITS, :] + r.acc_m[TRAITS : 2 * TRAITS, :]
        mine = r.mk.at[step, z]
        to_snp(lambda k: mine, lambda k: mine, r.mk_ssem.at[step], lambda k: r.mk_rsem.at[step], order)

    first_animal = c * slots

    def one_hot(index):
        local = index - first_animal
        high = jnp.bitwise_and(local, HI - 1)
        low = jnp.right_shift(local, 8)
        n = index.shape[1]
        hot = (lax.broadcasted_iota(jnp.int32, (HI, n), 0) == high).astype(F32).astype(BF16)
        here = jnp.logical_and(low >= 0, low < lows)
        around_low = jnp.bitwise_and(low + (reach - z) * (lows // nz), lows - 1)
        place = jnp.where(here, around_low, -8)
        return hot, place - jnp.right_shift(lax.broadcasted_iota(jnp.int32, (8, n), 0), 2)

    def load_field(step, which):
        first, count = which
        high, low = split(r.field[step, first : first + count, :])
        r.field_bf[2 * first : 2 * first + count, :] = high
        r.field_bf[2 * first + count : 2 * (first + count), :] = low

    def gather(which, hot, key):
        first, count = which
        picked = jnp.dot(
            r.field_bf[2 * first : 2 * (first + count), :], hot, preferred_element_type=F32
        )
        total = jnp.zeros((8, hot.shape[1]), F32)
        for g in range(count // 8):
            value = picked[g * 8 : g * 8 + 8, :] + picked[count + g * 8 : count + g * 8 + 8, :]
            total = total + jnp.where(key == 2 * (g + first // 8), value, 0.0)
        return total

    def gather_all(which, l):
        return gather(which, r.hot[2 * l], r.key[2 * l]) + gather(which, r.hot[2 * l + 1], r.key[2 * l + 1])

    def halves(total):
        return total[0:TRAITS, :] + total[TRAITS:8, :]

    def scatter(which, value, hot, key):
        first, count = which
        high, low = split(jnp.concatenate([value, value], axis=0))
        pieces = []
        for piece in (high.astype(F32), low.astype(F32)):
            for g in range(count // 8):
                pieces.append(jnp.where(key == 2 * (g + first // 8), piece, 0.0))
        spread = jnp.concatenate(pieces, axis=0).astype(BF16)
        return lax.dot_general(spread, hot, (((1,), (1,)), ((), ())), preferred_element_type=F32)

    def slots_of(block):
        return jnp.concatenate([block[i : i + TRAITS, :] for i in range(0, prow, TRAITS)], axis=1)

    readers = (((-2, 5), (-1, 3)), ((1, 0), (-1, 4)), ((2, 1), (1, 2)))

    def send_sums_up(step, l):
        def to(readers_l):
            for offset, place_there in readers_l:
                send(
                    r.up_own.at[step, l], r.up_recv.at[step, place_there],
                    r.up_ssem.at[step], r.up_rsem.at[step, place_there // 2], (cohort_at(offset), z),
                )

        if isinstance(l, int):
            to(readers[l])
        else:
            for i in range(SPAN):
                pl.when(l == i)(functools.partial(to, readers[i]))

    def send_own(step, src):
        for l in reversed(range(SPAN)):
            send(
                src, r.own_recv.at[step, l], r.own_ssem.at[step], r.own_rsem.at[step], (cohort_at(-(l + 1)), z)
            )

    def factor_of(sire, dam):
        known = jnp.where(sire >= 0, 1.0, 0.0) + jnp.where(dam >= 0, 1.0, 0.0)
        return 4.0 / (4.0 - known)

    row4 = lax.broadcasted_iota(jnp.int32, (4, 128), 0)
    at_owner = jnp.where(is_owner, 1.0, 0.0)
    whole = (0, rows)

    send_own(0, r.z_a0.at[:, my_slots])
    for load in loads[3:]:
        load.wait()
    gen_inv, res_inv, coup, prior = (x[...] for x in (r.gen_inv, r.res_inv, r.coup, r.prior))

    for step in range(2):
        if step == 0:
            marker_product(0)
            load_field(0, whole)

            @pl.loop(0, SPAN)
            def _(i):
                l = SPAN - 1 - i
                wait(r.idx_recv.at[l], r.idx_rsem.at[l])
                for k in range(2):
                    hot, key = one_hot(r.idx_recv[l, k])
                    r.hot[2 * l + k] = hot
                    r.key[2 * l + k] = key
                r.up_own[0, l] = halves(gather_all(whole, l))
                send_sums_up(0, l)
                r.factor[l] = factor_of(r.idx_recv[l, 0], r.idx_recv[l, 1])

            hot, key = one_hot(r.geno_idx[...])
            r.hot_g[...] = hot
            r.key_g[...] = key
        else:
            @pl.when(is_owner)
            def _():
                wait(r.z_s.at[1, :, pl.ds(0, (owners - 1) * OWN)], r.zs_rsem)

            @pl.when(jnp.logical_not(is_owner))
            def _():
                wait(r.z_s.at[1], r.zs_rsem)

            marker_product(1)

            wait(r.field.at[1, pl.ds(0, rows - prow), :], r.fl_rsem)
            load_field(1, whole)

            @pl.loop(0, SPAN)
            def _(i):
                l = SPAN - 1 - i
                total = gather_all(whole, l)
                r.up_own[1, l] = halves(total)
                send_sums_up(1, l)

            to_snp(
                lambda k: r.image_a, lambda k: r.q_a.at[:, my_slots], r.qa_ssem, lambda k: r.qa_rsem, order
            )
            r.q_a[:, my_slots] = r.image_a[...]

            @pl.when(is_owner)
            def _():
                r.q_s[:, own_at] = r.image_s[...]
                mine = r.q_s.at[:, own_at]
                to_cohort(mine, mine, r.qs_ssem, r.qs_rsem)

        dir_g = halves(gather(whole, r.hot_g[...], r.key_g[...]))

        def tie_up():
            wait(r.mk.at[step, pl.ds(0, nz - 1)], r.mk_rsem.at[step])
            mismatch = dir_g - jnp.sum(r.mk[step], axis=0)
            tied = mix(coup, mismatch)

            both = stacked_split(tied)

            @pl.loop(0, chunks)
            def _(j):
                at = pl.ds(pl.multiple_of(j * chunk, chunk), chunk)
                sums = jnp.dot(both, r.geno_hi[j], preferred_element_type=F32) + jnp.dot(
                    both, r.geno_lo[j], preferred_element_type=F32
                )
                r.part_s[step, :, at] = sums[0:TRAITS, :] + sums[TRAITS : 2 * TRAITS, :]

            r.sum_s[step, c] = r.part_s[step, :, own_at]

            def send_sums(other):
                @pl.when(other < owners)
                def _():
                    send(
                        r.part_s.at[step, :, pl.ds(pl.multiple_of(other * OWN, OWN), OWN)],
                        r.sum_s.at[step, c], r.ss_ssem.at[step], r.ss_rsem.at[step], (other, z),
                    )

            if step == 0:
                around(send_sums)
            return mismatch, tied, send_sums

        if step == 0:
            mismatch, tied, send_sums = tie_up()

        wait(r.own_recv.at[step], r.own_rsem.at[step])
        def form(l):
            wait(r.up_recv.at[step, pl.ds(0, 2)], r.up_rsem.at[step, l])
            parents = r.up_own[step, l] + r.up_recv[step, 2 * l] + r.up_recv[step, 2 * l + 1]
            apart_l = r.own_recv[step, l] - 0.5 * parents
            mixed_l = mix(gen_inv, r.factor[l] * apart_l)
            r.terms[l] = -0.5 * mixed_l
            return apart_l, mixed_l

        deviation, mixed = form(0)
        r.mixed[step] = mixed
        send(
            r.mixed.at[step], r.down_recv.at[step],
            r.down_ssem.at[step], r.down_rsem.at[step], (cohort_at(1), z),
        )

        own = r.z_a0[:, my_slots] if step == 0 else r.y_own[...]
        local_a = r.weight[...] * mix(res_inv, own)
        own_s = r.z_s[step, :, own_at]
        local_s = mix(prior, own_s)
        if step == 0:
            r.local_s[...] = local_s
            r.deviation[...] = deviation
            curve = fold(own * local_a + deviation * mixed) + at_owner * fold(own_s * local_s)
            gamma_row = fold(own * r.res_a0[:, my_slots]) + at_owner * fold(own_s * r.rhs_s[:, own_at])
            cross_row = jnp.zeros((1, 128), F32)
        else:
            wait(r.dot_c.at[0, pl.ds(0, nc - 1)], r.dc_rsem.at[0])
            dots = jnp.sum(r.dot_c[0], axis=0)
            gamma0, delta0 = total_of(dots[0:1, :]), total_of(dots[1:2, :])
            alpha0 = gamma0 / delta0
            z_own = r.z_a0[:, my_slots] - alpha0 * own
            res_a1 = r.res_a0[:, my_slots] - alpha0 * r.image_a[...]
            zs_own = r.z_s[0, :, own_at] - alpha0 * own_s
            res_s1 = r.rhs_s[:, own_at] - alpha0 * r.image_s[...]
            gamma_row = fold(z_own * res_a1) + at_owner * fold(zs_own * res_s1)
            cross_row = fold(z_own * r.image_a[...]) + at_owner * fold(zs_own * r.image_s[...])
            deviation = r.deviation[...] - alpha0 * deviation
            z_mixed = mix(gen_inv, r.factor[0] * deviation)
            record = r.weight[...] * mix(res_inv, z_own)
            curve = fold(z_own * record + deviation * z_mixed) + at_owner * fold(
                zs_own * (r.local_s[...] - alpha0 * local_s)
            )
        r.dot_z[step, z] = jnp.where(
            row4 == 0, gamma_row, jnp.where(row4 == 1, curve, jnp.where(row4 == 2, cross_row, 0.0))
        )
        my_dots = r.dot_z.at[step, z]
        to_snp(lambda k: my_dots, lambda k: my_dots, r.dz_ssem.at[step], lambda k: r.dz_rsem.at[step], order)

        r.acc_b[...] = jnp.zeros_like(r.acc_b)

        @pl.loop(0, SPAN)
        def _(l):
            @pl.when(l > 0)
            def _():
                form(l)

            r.acc_b[...] += scatter(whole, r.terms[l], r.hot[2 * l], r.key[2 * l]) + scatter(
                whole, r.terms[l], r.hot[2 * l + 1], r.key[2 * l + 1]
            )

        r.back[step] = r.acc_b[0:rows, :] + r.acc_b[rows : 2 * rows, :]
        to_snp(
            lambda k: r.back.at[step, pl.ds((k + reach) % nz * prow, prow), :],
            lambda k: r.back_recv.at[step, k], r.bk_ssem.at[step], lambda k: r.bk_rsem.at[step], order,
        )
        r.back_recv[step, 0] = r.back[step, my_rows, :]

        if step == 1:
            mismatch, tied, send_sums = tie_up()
            around(send_sums)
        def send_dots():
            if step == 0:
                r.mismatch[...] = mismatch
                tied_row = fold(mismatch * tied)
            else:
                apart = r.mismatch[...] - alpha0 * mismatch
                tied_row = fold(apart * mix(coup, apart))
            wait(r.dot_z.at[step, pl.ds(0, nz - 1)], r.dz_rsem.at[step])
            r.dot_c[step, c] = jnp.sum(r.dot_z[step], axis=0) + jnp.where(row4 == 1, tied_row, 0.0)
            my_dots = r.dot_c.at[step, c]
            to_cohort(my_dots, my_dots, r.dc_ssem.at[step], r.dc_rsem.at[step])

        if step == 1:
            send_dots()

        def markers():
            @pl.when(is_owner)
            def _():
                wait(r.sum_s.at[step, pl.ds(0, nc - 1)], r.ss_rsem.at[step])

            image_s = local_s - jnp.sum(jnp.where(is_owner, r.sum_s[step], 0.0), axis=0)
            if step == 0:
                r.image_s[...] = image_s
                y_s = precond_s(image_s, own_at)

                @pl.when(is_owner)
                def _():
                    r.z_s[1, :, own_at] = y_s
                    mine = r.z_s.at[1, :, own_at]
                    to_cohort(mine, mine, r.zs_ssem, r.zs_rsem)
            else:

                @pl.when(is_owner)
                def _():
                    r.ws_own[...] = image_s
                    landing = r.out_w_s.at[:, own_at]
                    to_cohort(r.ws_own, landing, r.rs_ssem, r.rs_rsem)
                    pltpu.make_async_copy(r.ws_own, landing, r.out_sem.at[6]).start()

        if step == 0:
            markers()

        tie = scatter((reach * prow, prow), tied, r.hot_g[...], r.key_g[...])
        local_a = local_a + slots_of(tie[0:prow, :] + tie[prow : 2 * prow, :])
        wait(r.down_recv.at[step], r.down_rsem.at[step])
        local_a = local_a + r.down_recv[step]
        wait(r.back_recv.at[step, pl.ds(0, nz - 1)], r.bk_rsem.at[step])
        image_a = local_a + slots_of(jnp.sum(r.back_recv[step], axis=0))
        if step == 0:
            y_a = precond_a(image_a)
            for i in range(0, prow, 8):
                lo = i // TRAITS
                at = reach * prow + i
                r.field[1, at : at + 8, :] = jnp.concatenate(
                    [y_a[:, lo * HI : (lo + 1) * HI], y_a[:, (lo + 1) * HI : (lo + 2) * HI]], axis=0
                )
            mine = r.field.at[1, my_rows, :]
            to_snp(
                lambda k: mine, lambda k: r.field.at[1, pl.ds((reach - k) % nz * prow, prow), :],
                r.fl_ssem, lambda k: r.fl_rsem, order,
            )
            r.y_own[...] = y_a
            r.image_a[...] = image_a
            send_own(1, r.y_own)
            send_dots()
        else:
            r.w_own[...] = image_a
            landing = r.out_w_a.at[:, my_slots]
            to_snp(lambda k: r.w_own, lambda k: landing, r.ra_ssem, lambda k: r.ra_rsem, order)
            pltpu.make_async_copy(r.w_own, landing, r.out_sem.at[5]).start()

        if step == 1:
            markers()

    wait(r.dot_c.at[1, pl.ds(0, nc - 1)], r.dc_rsem.at[1])
    dots = jnp.sum(r.dot_c[1], axis=0)
    gamma1, delta_z, cross = (total_of(dots[i : i + 1, :]) for i in range(3))
    beta = gamma1 / gamma0
    alpha1 = gamma1 / (delta_z + 2.0 * beta * cross + beta * beta * delta0)

    once = alpha0 + alpha1 * (1.0 + beta)
    twice = alpha1 * alpha0
    wait(r.q_a.at[:, pl.ds(0, slots - part)], r.qa_rsem)

    @pl.loop(0, lows // 2, unroll=4)
    def _(j):
        here = pl.ds(pl.multiple_of(j * 2 * HI, 2 * HI), 2 * HI)
        y = r.field[1, place_of(j), :]
        y = jnp.concatenate([y[0:TRAITS, :], y[TRAITS:8, :]], axis=1)
        r.sol_a[:, here] = once * r.z_a0[:, here] - twice * y
        r.left_a[:, here] = r.res_a0[:, here] - once * r.q_a[:, here]

    def arrived(full, sem):
        @pl.when(is_owner)
        def _():
            wait(full.at[:, pl.ds(0, (owners - 1) * OWN)], sem)

        @pl.when(jnp.logical_not(is_owner))
        def _():
            wait(full, sem)

    arrived(r.q_s, r.qs_rsem)

    @pl.loop(0, owners, unroll=5)
    def _(j):
        here = pl.ds(pl.multiple_of(j * OWN, OWN), OWN)
        r.sol_s[:, here] = once * r.z_s[0, :, here] - twice * r.z_s[1, :, here]
        r.left_s[:, here] = r.rhs_s[:, here] - once * r.q_s[:, here]

    r.scale[...] = jnp.broadcast_to(twice, r.scale.shape)
    stores = [
        pltpu.make_async_copy(src, dst, r.out_sem.at[i])
        for i, (src, dst) in enumerate(
            (
                (r.sol_a, r.out_sol_a), (r.sol_s, r.out_sol_s), (r.left_a, r.out_left_a),
                (r.left_s, r.out_left_s), (r.scale, r.out_scale),
            )
        )
    ]
    for store in stores:
        store.start()

    for l in range(SPAN):
        wait(r.idx_recv.at[l], r.idx_ssem.at[l])
    for step in range(2):
        wait(r.up_recv.at[step], r.up_ssem.at[step])
        wait(r.own_recv.at[step], r.own_ssem.at[step])
        wait(r.mixed.at[step], r.down_ssem.at[step])
        wait(r.mk.at[step, pl.ds(0, nz - 1)], r.mk_ssem.at[step])
        wait(r.dot_z.at[step, pl.ds(0, nz - 1)], r.dz_ssem.at[step])
        wait(r.dot_c.at[step, pl.ds(0, nc - 1)], r.dc_ssem.at[step])
        wait(r.back_recv.at[step, pl.ds(0, nz - 1)], r.bk_ssem.at[step])

        @pl.when(is_owner)
        def _():
            wait(r.part_s.at[step, :, pl.ds(0, (owners - 1) * OWN)], r.ss_ssem.at[step])

        @pl.when(jnp.logical_not(is_owner))
        def _():
            wait(r.part_s.at[step], r.ss_ssem.at[step])

    @pl.when(is_owner)
    def _():
        for sem in (r.zs_ssem, r.qs_ssem, r.rs_ssem):
            wait(r.sum_s.at[0, pl.ds(0, nc - 1)], sem)

    wait(r.field.at[1, pl.ds(0, rows - prow), :], r.fl_ssem)
    wait(r.q_a.at[:, pl.ds(0, slots - part)], r.qa_ssem)
    wait(r.q_a.at[:, pl.ds(0, slots - part)], r.ra_ssem)
    for store in stores:
        store.wait()
    pltpu.make_async_copy(r.w_own, r.out_w_a.at[:, my_slots], r.out_sem.at[5]).wait()
    wait(r.sol_a.at[:, pl.ds(0, slots - part)], r.ra_rsem)

    @pl.when(is_owner)
    def _():
        pltpu.make_async_copy(r.ws_own, r.out_w_s.at[:, own_at], r.out_sem.at[6]).wait()

    arrived(r.sol_s, r.rs_rsem)


def place(sol_a, sol_s, left_a, left_s, w_a, w_s, scale, out_sol_a, out_sol_s, out_ra, out_rs):
    twice = scale[0:1, 0:1]
    out_sol_a[...] = sol_a[...]
    out_sol_s[...] = sol_s[...]
    out_ra[...] = left_a[...] + twice * w_a[...]
    out_rs[...] = left_s[...] + twice * w_s[...]


def body(nc, nz, rhs_a, rhs_s, weight, sire, dam, sizes, geno_idx, genotypes, pre_a, pre_s, *small):
    slots, snps, genos = rhs_a.shape[1], rhs_s.shape[1], geno_idx.shape[0]
    part = slots // nz
    rows = slots // HI * TRAITS
    chunk, chunks = snps, 1
    vmem, dma = pltpu.VMEM, pltpu.SemaphoreType.DMA
    inputs = dict(
        rhs_a=rhs_a, rhs_s=rhs_s, weight=weight[None], sire=sire[None], dam=dam[None], sizes=sizes[None],
        geno_idx=geno_idx[None], genotypes=genotypes, pre_a=pre_a, pre_s=pre_s,
        gen_inv=small[0], res_inv=small[1], coup=small[2], prior=small[3],
    )
    scratch = dict(
        rhs_a=vmem(rhs_a.shape, F32),
        rhs_s=vmem(rhs_s.shape, F32),
        weight=vmem((1, part), F32),
        sizes=vmem((1, nc), jnp.int32),
        geno_idx=vmem((1, genos), jnp.int32),
        pre_a=vmem(pre_a.shape, F32),
        pre_s=vmem(pre_s.shape, F32),
        gen_inv=vmem((TRAITS, TRAITS), F32),
        res_inv=vmem((TRAITS, TRAITS), F32),
        coup=vmem((TRAITS, TRAITS), F32),
        prior=vmem((TRAITS, TRAITS), F32),
        geno_f32=vmem((chunks, genos, chunk), F32),
        geno_hi=vmem((chunks, genos, chunk), BF16),
        geno_lo=vmem((chunks, genos, chunk), BF16),
        idx_recv=vmem((SPAN, 2, 1, part), jnp.int32),
        hot=vmem((2 * SPAN, HI, part), BF16),
        key=vmem((2 * SPAN, 8, part), jnp.int32),
        hot_g=vmem((HI, genos), BF16),
        key_g=vmem((8, genos), jnp.int32),
        res_a0=vmem((TRAITS, slots), F32),
        z_a0=vmem((TRAITS, slots), F32),
        field=vmem((2, rows, HI), F32),
        field_bf=vmem((2 * rows, HI), BF16),
        z_s=vmem((2, TRAITS, snps), F32),
        acc_m=vmem((2 * TRAITS, genos), F32),
        mk=vmem((2, nz, TRAITS, genos), F32),
        part_s=vmem((2, TRAITS, snps), F32),
        sum_s=vmem((2, nc, TRAITS, OWN), F32),
        factor=vmem((SPAN, 1, part), F32),
        up_own=vmem((2, SPAN, TRAITS, part), F32),
        up_recv=vmem((2, 6, TRAITS, part), F32),
        mixed=vmem((2, TRAITS, part), F32),
        down_recv=vmem((2, TRAITS, part), F32),
        own_recv=vmem((2, SPAN, TRAITS, part), F32),
        terms=vmem((SPAN, TRAITS, part), F32),
        dot_z=vmem((2, nz, 4, 128), F32),
        dot_c=vmem((2, nc, 4, 128), F32),
        acc_b=vmem((2 * rows, HI), F32),
        back=vmem((2, rows, HI), F32),
        back_recv=vmem((2, nz, rows // nz, HI), F32),
        image_a=vmem((TRAITS, part), F32),
        y_own=vmem((TRAITS, part), F32),
        w_own=vmem((TRAITS, part), F32),
        deviation=vmem((TRAITS, part), F32),
        mismatch=vmem((TRAITS, genos), F32),
        local_s=vmem((TRAITS, OWN), F32),
        image_s=vmem((TRAITS, OWN), F32),
        q_a=vmem((TRAITS, slots), F32),
        sol_a=vmem((TRAITS, slots), F32),
        left_a=vmem((TRAITS, slots), F32),
        q_s=vmem((TRAITS, snps), F32),
        ws_own=vmem((TRAITS, OWN), F32),
        sol_s=vmem((TRAITS, snps), F32),
        left_s=vmem((TRAITS, snps), F32),
        scale=vmem((8, 128), F32),
        out_sem=dma((7,)),
        load_sem=dma((11 + chunks,)),
    )
    for name, shape in dict(
        idx=(SPAN,), own=(2,), down=(2,), mk=(2,), ss=(2,), dz=(2,), dc=(2,), bk=(2,), zs=(), rs=(), qs=(), qa=(), fl=(), ra=(),
    ).items():
        scratch[name + "_ssem"] = dma(shape)
        scratch[name + "_rsem"] = dma(shape)
    scratch |= dict(up_ssem=dma((2,)), up_rsem=dma((2, SPAN)))
    names = ["in_" + name for name in inputs]
    names += ["out_sol_a", "out_sol_s", "out_left_a", "out_left_s", "out_w_a", "out_w_s", "out_scale"] + list(scratch)
    outs = [jax.ShapeDtypeStruct(x.shape, F32) for x in (rhs_a, rhs_s, rhs_a, rhs_s)]
    limit = 56 * 1024 * 1024
    results = pl.pallas_call(
        functools.partial(kernel, nc, nz, names),
        out_shape=outs + outs[:2] + [jax.ShapeDtypeStruct((8, 128), F32)],
        in_specs=[pl.BlockSpec(memory_space=pl.ANY)] * len(inputs),
        out_specs=[pl.BlockSpec(memory_space=pl.ANY)] * 7,
        scratch_shapes=list(scratch.values()),
        compiler_params=pltpu.CompilerParams(collective_id=0, has_side_effects=True, vmem_limit_bytes=limit),
        cost_estimate=pl.CostEstimate(flops=4 * 10**9, bytes_accessed=10**7, transcendentals=0),
    )(*inputs.values())
    return pl.pallas_call(
        place,
        out_shape=outs,
        in_specs=[pl.BlockSpec(memory_space=pltpu.VMEM)] * 7,
        out_specs=[pl.BlockSpec(memory_space=pltpu.VMEM)] * 4,
    )(*results)


def solution(mesh):
    nc, nz = mesh.shape["cohort"], mesh.shape["snp"]
    in_specs = (
        P(None, "cohort"),
        P(None, "snp"),
        P("cohort"),
        P("cohort"),
        P("cohort"),
        P(),
        P("cohort"),
        P("cohort", "snp"),
        P(None, None, "cohort"),
        P(None, None, "snp"),
        P(),
        P(),
        P(),
        P(),
    )
    out_specs = (P(None, "cohort"), P(None, "snp"), P(None, "cohort"), P(None, "snp"))
    return jax.shard_map(
        functools.partial(body, nc, nz), mesh=mesh, in_specs=in_specs, out_specs=out_specs, check_vma=False
    )
```

```python
import functools
import types

import jax
import jax.numpy as jnp
from jax import lax
from jax.experimental import pallas as pl
from jax.experimental.pallas import tpu as pltpu
from jax.sharding import PartitionSpec as P

SPAN = 3
TRAITS = 4
HI = 256
OWN = 256
F32 = jnp.float32
BF16 = jnp.bfloat16
MESH = pl.DeviceIdType.MESH


def split(x):
    high = x.astype(BF16)
    return high, (x - high.astype(F32)).astype(BF16)


def stacked_split(x):
    high, low = split(x)
    return jnp.concatenate([high.astype(F32), low.astype(F32)], axis=0).astype(BF16)


def mix(matrix, field):
    total = matrix[:, 0:1] * field[0:1, :]
    for u in range(1, TRAITS):
        total = total + matrix[:, u : u + 1] * field[u : u + 1, :]
    return total


def fold(x):
    total = x[:, 0:128]
    for i in range(1, x.shape[1] // 128):
        total = total + x[:, i * 128 : (i + 1) * 128]
    return jnp.sum(total, axis=0, keepdims=True)


def total_of(row):
    return jnp.sum(row, axis=1, keepdims=True)


def z_plan(nz):
    order = sorted(range(1, nz), key=lambda k: -min(k, nz - k))
    return order, nz // 4


def kernel(nc, nz, names, *refs):
    r = types.SimpleNamespace(**dict(zip(names, refs)))
    c = lax.axis_index("cohort")
    z = lax.axis_index("snp")
    slots = r.rhs_a.shape[1]
    part = slots // nz
    lows = slots // HI
    rows = lows * TRAITS
    prow = rows // nz
    snps = r.rhs_s.shape[1]
    owners = snps // OWN
    chunk = r.geno_f32.shape[2]
    chunks = snps // chunk
    own_block = lax.rem(c, owners)
    is_owner = c < owners
    own_at = pl.ds(pl.multiple_of(own_block * OWN, OWN), OWN)
    my_slots = pl.ds(pl.multiple_of(z * part, part), part)
    order, reach = z_plan(nz)
    my_rows = slice(reach * prow, (reach + 1) * prow)

    def cohort_at(k):
        return lax.rem(c + k + nc, nc)

    def send(src, dst, send_sem, recv_sem, device):
        pltpu.make_async_remote_copy(
            src_ref=src, dst_ref=dst, send_sem=send_sem, recv_sem=recv_sem,
            device_id=device, device_id_type=MESH,
        ).start()

    def wait(ref, sem):
        pltpu.make_async_copy(ref, ref, sem).wait()

    loads = []
    for src, dst in (
        (r.in_rhs_a, r.rhs_a),
        (r.in_pre_a, r.pre_a),
        (r.in_sizes, r.sizes),
        (r.in_geno_idx, r.geno_idx),
        (r.in_rhs_s, r.rhs_s),
        (r.in_pre_s, r.pre_s),
        (r.in_weight.at[:, my_slots], r.weight),
        (r.in_gen_inv, r.gen_inv),
        (r.in_res_inv, r.res_inv),
        (r.in_coup, r.coup),
        (r.in_prior, r.prior),
    ):
        loads.append(pltpu.make_async_copy(src, dst, r.load_sem.at[len(loads)]))
    for j in range(chunks):
        loads.append(
            pltpu.make_async_copy(
                r.in_genotypes.at[:, j * chunk : (j + 1) * chunk], r.geno_f32.at[j], r.load_sem.at[len(loads)]
            )
        )
    for load in loads:
        load.start()

    barrier = pltpu.get_barrier_semaphore()

    @pl.loop(1, nz)
    def _(k):
        pl.semaphore_signal(barrier, inc=1, device_id=(c, lax.rem(z + k, nz)), device_id_type=MESH)

    @pl.loop(1, nc)
    def _(k):
        pl.semaphore_signal(barrier, inc=1, device_id=(cohort_at(k), z), device_id_type=MESH)

    pl.semaphore_wait(barrier, nz - 1 + nc - 1)

    for l in range(SPAN):
        for k, src in enumerate((r.in_sire, r.in_dam)):
            send(
                src.at[:, my_slots], r.idx_recv.at[l, k], r.idx_ssem.at[l], r.idx_rsem.at[l],
                (cohort_at(-(l + 1)), z),
            )

    def to_snp(src_of, dst_of, send_sem, recv_sem_of, ks):
        for k in ks:
            send(src_of(k), dst_of(k), send_sem, recv_sem_of(k), (c, lax.rem(z + k, nz)))

    def around(act):
        ny = min(4, nc // 2)
        nx = nc // (2 * ny)
        x, y, core = c // (2 * ny), c // 2 % ny, c % 2
        ys = [lax.rem(y + (j + ny // 2) % ny, ny) * 2 for j in range(ny)]

        @pl.loop(0, nx)
        def _(i):
            to_x = lax.rem(x + i + nx // 2, nx) * (2 * ny)
            for j in range(ny):
                for to_core in (core, 1 - core):
                    other = to_x + ys[j] + to_core
                    if to_core is core and (j + ny // 2) % ny == 0:
                        pl.when(other != c)(functools.partial(act, other))
                    else:
                        act(other)

    def to_cohort(src, dst, send_sem, recv_sem):
        around(lambda other: send(src, dst, send_sem, recv_sem, (other, z)))

    for load in loads[:3]:
        load.wait()

    cohort_row = lax.broadcasted_iota(jnp.int32, (1, nc), 1)
    live_count = total_of(jnp.where(cohort_row == c, r.sizes[...].astype(F32), 0.0))

    def place_of(j):
        at = lax.rem(j + lows // 2 - z * (prow // 8) + reach * (prow // 8), lows // 2)
        return pl.ds(pl.multiple_of(at * 8, 8), 8)

    @pl.loop(0, lows // 2, unroll=4)
    def _(j):
        here = pl.ds(pl.multiple_of(j * 2 * HI, 2 * HI), 2 * HI)
        slot = (lax.broadcasted_iota(jnp.int32, (1, 2 * HI), 1) + j * 2 * HI).astype(F32)
        res = jnp.where(slot < live_count, r.rhs_a[:, here], 0.0)
        r.res_a0[:, here] = res
        pre = r.pre_a[0, :, here] * res[0:1, :]
        for u in range(1, TRAITS):
            pre = pre + r.pre_a[u, :, here] * res[u : u + 1, :]
        r.z_a0[:, here] = pre
        r.field[0, place_of(j), :] = jnp.concatenate([pre[:, :HI], pre[:, HI:]], axis=0)

    def precond_s(res, at):
        pre = r.pre_s[0, :, at] * res[0:1, :]
        for u in range(1, TRAITS):
            pre = pre + r.pre_s[u, :, at] * res[u : u + 1, :]
        return pre

    def precond_a(res):
        pre = r.pre_a[0, :, my_slots] * res[0:1, :]
        for u in range(1, TRAITS):
            pre = pre + r.pre_a[u, :, my_slots] * res[u : u + 1, :]
        return pre

    def marker_product(step):
        r.acc_m[...] = jnp.zeros_like(r.acc_m)

        @pl.loop(0, chunks)
        def _(j):
            at = pl.ds(pl.multiple_of(j * chunk, chunk), chunk)
            if step == 0:
                z_s = precond_s(r.rhs_s[:, at], at)
                r.z_s[0, :, at] = z_s
                high, low = split(r.geno_f32[j])
                r.geno_hi[j] = high
                r.geno_lo[j] = low
            else:
                z_s = r.z_s[step, :, at]
                high, low = r.geno_hi[j], r.geno_lo[j]
            both = stacked_split(z_s)
            dims = (((1,), (1,)), ((), ()))
            r.acc_m[...] += lax.dot_general(
                both, high, dims, preferred_element_type=F32
            ) + lax.dot_general(both, low, dims, preferred_element_type=F32)

        r.mk[step, z] = r.acc_m[0:TRAITS, :] + r.acc_m[TRAITS : 2 * TRAITS, :]
        mine = r.mk.at[step, z]
        to_snp(lambda k: mine, lambda k: mine, r.mk_ssem.at[step], lambda k: r.mk_rsem.at[step], order)

    first_animal = c * slots

    def one_hot(index):
        local = index - first_animal
        high = jnp.bitwise_and(local, HI - 1)
        low = jnp.right_shift(local, 8)
        n = index.shape[1]
        hot = (lax.broadcasted_iota(jnp.int32, (HI, n), 0) == high).astype(F32).astype(BF16)
        here = jnp.logical_and(low >= 0, low < lows)
        around_low = jnp.bitwise_and(low + (reach - z) * (lows // nz), lows - 1)
        place = jnp.where(here, around_low, -8)
        return hot, place - jnp.right_shift(lax.broadcasted_iota(jnp.int32, (8, n), 0), 2)

    def load_field(step, which):
        first, count = which
        high, low = split(r.field[step, first : first + count, :])
        r.field_bf[2 * first : 2 * first + count, :] = high
        r.field_bf[2 * first + count : 2 * (first + count), :] = low

    def gather(which, hot, key):
        first, count = which
        picked = jnp.dot(
            r.field_bf[2 * first : 2 * (first + count), :], hot, preferred_element_type=F32
        )
        total = jnp.zeros((8, hot.shape[1]), F32)
        for g in range(count // 8):
            value = picked[g * 8 : g * 8 + 8, :] + picked[count + g * 8 : count + g * 8 + 8, :]
            total = total + jnp.where(key == 2 * (g + first // 8), value, 0.0)
        return total

    def gather_all(which, l):
        return gather(which, r.hot[2 * l], r.key[2 * l]) + gather(which, r.hot[2 * l + 1], r.key[2 * l + 1])

    def halves(total):
        return total[0:TRAITS, :] + total[TRAITS:8, :]

    def scatter(which, value, hot, key):
        first, count = which
        high, low = split(jnp.concatenate([value, value], axis=0))
        pieces = []
        for piece in (high.astype(F32), low.astype(F32)):
            for g in range(count // 8):
                pieces.append(jnp.where(key == 2 * (g + first // 8), piece, 0.0))
        spread = jnp.concatenate(pieces, axis=0).astype(BF16)
        return lax.dot_general(spread, hot, (((1,), (1,)), ((), ())), preferred_element_type=F32)

    def slots_of(block):
        return jnp.concatenate([block[i : i + TRAITS, :] for i in range(0, prow, TRAITS)], axis=1)

    readers = (((-2, 5), (-1, 3)), ((1, 0), (-1, 4)), ((2, 1), (1, 2)))

    def send_sums_up(step, l):
        def to(readers_l):
            for offset, place_there in readers_l:
                send(
                    r.up_own.at[step, l], r.up_recv.at[step, place_there],
                    r.up_ssem.at[step], r.up_rsem.at[step, place_there // 2], (cohort_at(offset), z),
                )

        if isinstance(l, int):
            to(readers[l])
        else:
            for i in range(SPAN):
                pl.when(l == i)(functools.partial(to, readers[i]))

    def send_own(step, src):
        for l in reversed(range(SPAN)):
            send(
                src, r.own_recv.at[step, l], r.own_ssem.at[step], r.own_rsem.at[step], (cohort_at(-(l + 1)), z)
            )

    def factor_of(sire, dam):
        known = jnp.where(sire >= 0, 1.0, 0.0) + jnp.where(dam >= 0, 1.0, 0.0)
        return 4.0 / (4.0 - known)

    row4 = lax.broadcasted_iota(jnp.int32, (4, 128), 0)
    at_owner = jnp.where(is_owner, 1.0, 0.0)
    whole = (0, rows)

    send_own(0, r.z_a0.at[:, my_slots])
    for load in loads[3:]:
        load.wait()
    gen_inv, res_inv, coup, prior = (x[...] for x in (r.gen_inv, r.res_inv, r.coup, r.prior))

    for step in range(2):
        if step == 0:
            marker_product(0)
            load_field(0, whole)

            @pl.loop(0, SPAN)
            def _(i):
                l = SPAN - 1 - i
                wait(r.idx_recv.at[l], r.idx_rsem.at[l])
                for k in range(2):
                    hot, key = one_hot(r.idx_recv[l, k])
                    r.hot[2 * l + k] = hot
                    r.key[2 * l + k] = key
                r.up_own[0, l] = halves(gather_all(whole, l))
                send_sums_up(0, l)
                r.factor[l] = factor_of(r.idx_recv[l, 0], r.idx_recv[l, 1])

            hot, key = one_hot(r.geno_idx[...])
            r.hot_g[...] = hot
            r.key_g[...] = key
        else:
            @pl.when(is_owner)
            def _():
                wait(r.z_s.at[1, :, pl.ds(0, (owners - 1) * OWN)], r.zs_rsem)

            @pl.when(jnp.logical_not(is_owner))
            def _():
                wait(r.z_s.at[1], r.zs_rsem)

            marker_product(1)

            wait(r.field.at[1, pl.ds(0, rows - prow), :], r.fl_rsem)
            load_field(1, whole)

            for l in reversed(range(SPAN)):
                total = gather_all(whole, l)
                r.up_own[1, l] = halves(total)
                send_sums_up(1, l)

            to_snp(
                lambda k: r.image_a, lambda k: r.q_a.at[:, my_slots], r.qa_ssem, lambda k: r.qa_rsem, order
            )
            r.q_a[:, my_slots] = r.image_a[...]

            @pl.when(is_owner)
            def _():
                r.q_s[:, own_at] = r.image_s[...]
                mine = r.q_s.at[:, own_at]
                to_cohort(mine, mine, r.qs_ssem, r.qs_rsem)

        dir_g = halves(gather(whole, r.hot_g[...], r.key_g[...]))

        def tie_up():
            wait(r.mk.at[step, pl.ds(0, nz - 1)], r.mk_rsem.at[step])
            mismatch = dir_g - jnp.sum(r.mk[step], axis=0)
            tied = mix(coup, mismatch)

            both = stacked_split(tied)

            @pl.loop(0, chunks)
            def _(j):
                at = pl.ds(pl.multiple_of(j * chunk, chunk), chunk)
                sums = jnp.dot(both, r.geno_hi[j], preferred_element_type=F32) + jnp.dot(
                    both, r.geno_lo[j], preferred_element_type=F32
                )
                r.part_s[step, :, at] = sums[0:TRAITS, :] + sums[TRAITS : 2 * TRAITS, :]

            r.sum_s[step, c] = r.part_s[step, :, own_at]

            def send_sums(other):
                @pl.when(other < owners)
                def _():
                    send(
                        r.part_s.at[step, :, pl.ds(pl.multiple_of(other * OWN, OWN), OWN)],
                        r.sum_s.at[step, c], r.ss_ssem.at[step], r.ss_rsem.at[step], (other, z),
                    )

            if step == 0:
                around(send_sums)
            return mismatch, tied, send_sums

        if step == 0:
            mismatch, tied, send_sums = tie_up()

        wait(r.own_recv.at[step], r.own_rsem.at[step])
        def form(l):
            wait(r.up_recv.at[step, pl.ds(0, 2)], r.up_rsem.at[step, l])
            parents = r.up_own[step, l] + r.up_recv[step, 2 * l] + r.up_recv[step, 2 * l + 1]
            apart_l = r.own_recv[step, l] - 0.5 * parents
            mixed_l = mix(gen_inv, r.factor[l] * apart_l)
            r.terms[l] = -0.5 * mixed_l
            return apart_l, mixed_l

        deviation, mixed = form(0)
        r.mixed[step] = mixed
        send(
            r.mixed.at[step], r.down_recv.at[step],
            r.down_ssem.at[step], r.down_rsem.at[step], (cohort_at(1), z),
        )

        own = r.z_a0[:, my_slots] if step == 0 else r.y_own[...]
        local_a = r.weight[...] * mix(res_inv, own)
        own_s = r.z_s[step, :, own_at]
        local_s = mix(prior, own_s)
        if step == 0:
            r.local_s[...] = local_s
            r.deviation[...] = deviation
            curve = fold(own * local_a + deviation * mixed) + at_owner * fold(own_s * local_s)
            gamma_row = fold(own * r.res_a0[:, my_slots]) + at_owner * fold(own_s * r.rhs_s[:, own_at])
            cross_row = jnp.zeros((1, 128), F32)
        else:
            wait(r.dot_c.at[0, pl.ds(0, nc - 1)], r.dc_rsem.at[0])
            dots = jnp.sum(r.dot_c[0], axis=0)
            gamma0, delta0 = total_of(dots[0:1, :]), total_of(dots[1:2, :])
            alpha0 = gamma0 / delta0
            z_own = r.z_a0[:, my_slots] - alpha0 * own
            res_a1 = r.res_a0[:, my_slots] - alpha0 * r.image_a[...]
            zs_own = r.z_s[0, :, own_at] - alpha0 * own_s
            res_s1 = r.rhs_s[:, own_at] - alpha0 * r.image_s[...]
            gamma_row = fold(z_own * res_a1) + at_owner * fold(zs_own * res_s1)
            cross_row = fold(z_own * r.image_a[...]) + at_owner * fold(zs_own * r.image_s[...])
            deviation = r.deviation[...] - alpha0 * deviation
            z_mixed = mix(gen_inv, r.factor[0] * deviation)
            record = r.weight[...] * mix(res_inv, z_own)
            curve = fold(z_own * record + deviation * z_mixed) + at_owner * fold(
                zs_own * (r.local_s[...] - alpha0 * local_s)
            )
        r.dot_z[step, z] = jnp.where(
            row4 == 0, gamma_row, jnp.where(row4 == 1, curve, jnp.where(row4 == 2, cross_row, 0.0))
        )
        my_dots = r.dot_z.at[step, z]
        to_snp(lambda k: my_dots, lambda k: my_dots, r.dz_ssem.at[step], lambda k: r.dz_rsem.at[step], order)

        r.acc_b[...] = jnp.zeros_like(r.acc_b)

        @pl.loop(0, SPAN)
        def _(l):
            @pl.when(l > 0)
            def _():
                form(l)

            r.acc_b[...] += scatter(whole, r.terms[l], r.hot[2 * l], r.key[2 * l]) + scatter(
                whole, r.terms[l], r.hot[2 * l + 1], r.key[2 * l + 1]
            )

        r.back[step] = r.acc_b[0:rows, :] + r.acc_b[rows : 2 * rows, :]
        to_snp(
            lambda k: r.back.at[step, pl.ds((k + reach) % nz * prow, prow), :],
            lambda k: r.back_recv.at[step, k], r.bk_ssem.at[step], lambda k: r.bk_rsem.at[step], order,
        )
        r.back_recv[step, 0] = r.back[step, my_rows, :]

        if step == 1:
            mismatch, tied, send_sums = tie_up()
            around(send_sums)
        def send_dots():
            if step == 0:
                r.mismatch[...] = mismatch
                tied_row = fold(mismatch * tied)
            else:
                apart = r.mismatch[...] - alpha0 * mismatch
                tied_row = fold(apart * mix(coup, apart))
            wait(r.dot_z.at[step, pl.ds(0, nz - 1)], r.dz_rsem.at[step])
            r.dot_c[step, c] = jnp.sum(r.dot_z[step], axis=0) + jnp.where(row4 == 1, tied_row, 0.0)
            my_dots = r.dot_c.at[step, c]
            to_cohort(my_dots, my_dots, r.dc_ssem.at[step], r.dc_rsem.at[step])

        if step == 1:
            send_dots()

        def markers():
            @pl.when(is_owner)
            def _():
                wait(r.sum_s.at[step, pl.ds(0, nc - 1)], r.ss_rsem.at[step])

            image_s = local_s - jnp.sum(jnp.where(is_owner, r.sum_s[step], 0.0), axis=0)
            if step == 0:
                r.image_s[...] = image_s
                y_s = precond_s(image_s, own_at)

                @pl.when(is_owner)
                def _():
                    r.z_s[1, :, own_at] = y_s
                    mine = r.z_s.at[1, :, own_at]
                    to_cohort(mine, mine, r.zs_ssem, r.zs_rsem)
            else:

                @pl.when(is_owner)
                def _():
                    r.ws_own[...] = image_s
                    landing = r.out_w_s.at[:, own_at]
                    to_cohort(r.ws_own, landing, r.rs_ssem, r.rs_rsem)
                    pltpu.make_async_copy(r.ws_own, landing, r.out_sem.at[6]).start()

        if step == 0:
            markers()

        tie = scatter((reach * prow, prow), tied, r.hot_g[...], r.key_g[...])
        local_a = local_a + slots_of(tie[0:prow, :] + tie[prow : 2 * prow, :])
        wait(r.down_recv.at[step], r.down_rsem.at[step])
        local_a = local_a + r.down_recv[step]
        wait(r.back_recv.at[step, pl.ds(0, nz - 1)], r.bk_rsem.at[step])
        image_a = local_a + slots_of(jnp.sum(r.back_recv[step], axis=0))
        if step == 0:
            y_a = precond_a(image_a)
            for i in range(0, prow, 8):
                lo = i // TRAITS
                at = reach * prow + i
                r.field[1, at : at + 8, :] = jnp.concatenate(
                    [y_a[:, lo * HI : (lo + 1) * HI], y_a[:, (lo + 1) * HI : (lo + 2) * HI]], axis=0
                )
            mine = r.field.at[1, my_rows, :]
            to_snp(
                lambda k: mine, lambda k: r.field.at[1, pl.ds((reach - k) % nz * prow, prow), :],
                r.fl_ssem, lambda k: r.fl_rsem, order,
            )
            r.y_own[...] = y_a
            r.image_a[...] = image_a
            send_own(1, r.y_own)
            send_dots()
        else:
            r.w_own[...] = image_a
            landing = r.out_w_a.at[:, my_slots]
            to_snp(lambda k: r.w_own, lambda k: landing, r.ra_ssem, lambda k: r.ra_rsem, order)
            pltpu.make_async_copy(r.w_own, landing, r.out_sem.at[5]).start()

        if step == 1:
            markers()

    wait(r.dot_c.at[1, pl.ds(0, nc - 1)], r.dc_rsem.at[1])
    dots = jnp.sum(r.dot_c[1], axis=0)
    gamma1, delta_z, cross = (total_of(dots[i : i + 1, :]) for i in range(3))
    beta = gamma1 / gamma0
    alpha1 = gamma1 / (delta_z + 2.0 * beta * cross + beta * beta * delta0)

    once = alpha0 + alpha1 * (1.0 + beta)
    twice = alpha1 * alpha0
    wait(r.q_a.at[:, pl.ds(0, slots - part)], r.qa_rsem)

    @pl.loop(0, lows // 2, unroll=4)
    def _(j):
        here = pl.ds(pl.multiple_of(j * 2 * HI, 2 * HI), 2 * HI)
        y = r.field[1, place_of(j), :]
        y = jnp.concatenate([y[0:TRAITS, :], y[TRAITS:8, :]], axis=1)
        r.sol_a[:, here] = once * r.z_a0[:, here] - twice * y
        r.left_a[:, here] = r.res_a0[:, here] - once * r.q_a[:, here]

    def arrived(full, sem):
        @pl.when(is_owner)
        def _():
            wait(full.at[:, pl.ds(0, (owners - 1) * OWN)], sem)

        @pl.when(jnp.logical_not(is_owner))
        def _():
            wait(full, sem)

    arrived(r.q_s, r.qs_rsem)

    @pl.loop(0, owners, unroll=5)
    def _(j):
        here = pl.ds(pl.multiple_of(j * OWN, OWN), OWN)
        r.sol_s[:, here] = once * r.z_s[0, :, here] - twice * r.z_s[1, :, here]
        r.left_s[:, here] = r.rhs_s[:, here] - once * r.q_s[:, here]

    r.scale[...] = jnp.broadcast_to(twice, r.scale.shape)
    stores = [
        pltpu.make_async_copy(src, dst, r.out_sem.at[i])
        for i, (src, dst) in enumerate(
            (
                (r.sol_a, r.out_sol_a), (r.sol_s, r.out_sol_s), (r.left_a, r.out_left_a),
                (r.left_s, r.out_left_s), (r.scale, r.out_scale),
            )
        )
    ]
    for store in stores:
        store.start()

    for l in range(SPAN):
        wait(r.idx_recv.at[l], r.idx_ssem.at[l])
    for step in range(2):
        wait(r.up_recv.at[step], r.up_ssem.at[step])
        wait(r.own_recv.at[step], r.own_ssem.at[step])
        wait(r.mixed.at[step], r.down_ssem.at[step])
        wait(r.mk.at[step, pl.ds(0, nz - 1)], r.mk_ssem.at[step])
        wait(r.dot_z.at[step, pl.ds(0, nz - 1)], r.dz_ssem.at[step])
        wait(r.dot_c.at[step, pl.ds(0, nc - 1)], r.dc_ssem.at[step])
        wait(r.back_recv.at[step, pl.ds(0, nz - 1)], r.bk_ssem.at[step])

        @pl.when(is_owner)
        def _():
            wait(r.part_s.at[step, :, pl.ds(0, (owners - 1) * OWN)], r.ss_ssem.at[step])

        @pl.when(jnp.logical_not(is_owner))
        def _():
            wait(r.part_s.at[step], r.ss_ssem.at[step])

    @pl.when(is_owner)
    def _():
        for sem in (r.zs_ssem, r.qs_ssem, r.rs_ssem):
            wait(r.sum_s.at[0, pl.ds(0, nc - 1)], sem)

    wait(r.field.at[1, pl.ds(0, rows - prow), :], r.fl_ssem)
    wait(r.q_a.at[:, pl.ds(0, slots - part)], r.qa_ssem)
    wait(r.q_a.at[:, pl.ds(0, slots - part)], r.ra_ssem)
    for store in stores:
        store.wait()
    pltpu.make_async_copy(r.w_own, r.out_w_a.at[:, my_slots], r.out_sem.at[5]).wait()
    wait(r.sol_a.at[:, pl.ds(0, slots - part)], r.ra_rsem)

    @pl.when(is_owner)
    def _():
        pltpu.make_async_copy(r.ws_own, r.out_w_s.at[:, own_at], r.out_sem.at[6]).wait()

    arrived(r.sol_s, r.rs_rsem)


def place(sol_a, sol_s, left_a, left_s, w_a, w_s, scale, out_sol_a, out_sol_s, out_ra, out_rs):
    twice = scale[0:1, 0:1]
    out_sol_a[...] = sol_a[...]
    out_sol_s[...] = sol_s[...]
    out_ra[...] = left_a[...] + twice * w_a[...]
    out_rs[...] = left_s[...] + twice * w_s[...]


def body(nc, nz, rhs_a, rhs_s, weight, sire, dam, sizes, geno_idx, genotypes, pre_a, pre_s, *small):
    slots, snps, genos = rhs_a.shape[1], rhs_s.shape[1], geno_idx.shape[0]
    part = slots // nz
    rows = slots // HI * TRAITS
    chunk, chunks = snps, 1
    vmem, dma = pltpu.VMEM, pltpu.SemaphoreType.DMA
    inputs = dict(
        rhs_a=rhs_a, rhs_s=rhs_s, weight=weight[None], sire=sire[None], dam=dam[None], sizes=sizes[None],
        geno_idx=geno_idx[None], genotypes=genotypes, pre_a=pre_a, pre_s=pre_s,
        gen_inv=small[0], res_inv=small[1], coup=small[2], prior=small[3],
    )
    scratch = dict(
        rhs_a=vmem(rhs_a.shape, F32),
        rhs_s=vmem(rhs_s.shape, F32),
        weight=vmem((1, part), F32),
        sizes=vmem((1, nc), jnp.int32),
        geno_idx=vmem((1, genos), jnp.int32),
        pre_a=vmem(pre_a.shape, F32),
        pre_s=vmem(pre_s.shape, F32),
        gen_inv=vmem((TRAITS, TRAITS), F32),
        res_inv=vmem((TRAITS, TRAITS), F32),
        coup=vmem((TRAITS, TRAITS), F32),
        prior=vmem((TRAITS, TRAITS), F32),
        geno_f32=vmem((chunks, genos, chunk), F32),
        geno_hi=vmem((chunks, genos, chunk), BF16),
        geno_lo=vmem((chunks, genos, chunk), BF16),
        idx_recv=vmem((SPAN, 2, 1, part), jnp.int32),
        hot=vmem((2 * SPAN, HI, part), BF16),
        key=vmem((2 * SPAN, 8, part), jnp.int32),
        hot_g=vmem((HI, genos), BF16),
        key_g=vmem((8, genos), jnp.int32),
        res_a0=vmem((TRAITS, slots), F32),
        z_a0=vmem((TRAITS, slots), F32),
        field=vmem((2, rows, HI), F32),
        field_bf=vmem((2 * rows, HI), BF16),
        z_s=vmem((2, TRAITS, snps), F32),
        acc_m=vmem((2 * TRAITS, genos), F32),
        mk=vmem((2, nz, TRAITS, genos), F32),
        part_s=vmem((2, TRAITS, snps), F32),
        sum_s=vmem((2, nc, TRAITS, OWN), F32),
        factor=vmem((SPAN, 1, part), F32),
        up_own=vmem((2, SPAN, TRAITS, part), F32),
        up_recv=vmem((2, 6, TRAITS, part), F32),
        mixed=vmem((2, TRAITS, part), F32),
        down_recv=vmem((2, TRAITS, part), F32),
        own_recv=vmem((2, SPAN, TRAITS, part), F32),
        terms=vmem((SPAN, TRAITS, part), F32),
        dot_z=vmem((2, nz, 4, 128), F32),
        dot_c=vmem((2, nc, 4, 128), F32),
        acc_b=vmem((2 * rows, HI), F32),
        back=vmem((2, rows, HI), F32),
        back_recv=vmem((2, nz, rows // nz, HI), F32),
        image_a=vmem((TRAITS, part), F32),
        y_own=vmem((TRAITS, part), F32),
        w_own=vmem((TRAITS, part), F32),
        deviation=vmem((TRAITS, part), F32),
        mismatch=vmem((TRAITS, genos), F32),
        local_s=vmem((TRAITS, OWN), F32),
        image_s=vmem((TRAITS, OWN), F32),
        q_a=vmem((TRAITS, slots), F32),
        sol_a=vmem((TRAITS, slots), F32),
        left_a=vmem((TRAITS, slots), F32),
        q_s=vmem((TRAITS, snps), F32),
        ws_own=vmem((TRAITS, OWN), F32),
        sol_s=vmem((TRAITS, snps), F32),
        left_s=vmem((TRAITS, snps), F32),
        scale=vmem((8, 128), F32),
        out_sem=dma((7,)),
        load_sem=dma((11 + chunks,)),
    )
    for name, shape in dict(
        idx=(SPAN,), own=(2,), down=(2,), mk=(2,), ss=(2,), dz=(2,), dc=(2,), bk=(2,), zs=(), rs=(), qs=(), qa=(), fl=(), ra=(),
    ).items():
        scratch[name + "_ssem"] = dma(shape)
        scratch[name + "_rsem"] = dma(shape)
    scratch |= dict(up_ssem=dma((2,)), up_rsem=dma((2, SPAN)))
    names = ["in_" + name for name in inputs]
    names += ["out_sol_a", "out_sol_s", "out_left_a", "out_left_s", "out_w_a", "out_w_s", "out_scale"] + list(scratch)
    outs = [jax.ShapeDtypeStruct(x.shape, F32) for x in (rhs_a, rhs_s, rhs_a, rhs_s)]
    limit = 56 * 1024 * 1024
    results = pl.pallas_call(
        functools.partial(kernel, nc, nz, names),
        out_shape=outs + outs[:2] + [jax.ShapeDtypeStruct((8, 128), F32)],
        in_specs=[pl.BlockSpec(memory_space=pl.ANY)] * len(inputs),
        out_specs=[pl.BlockSpec(memory_space=pl.ANY)] * 7,
        scratch_shapes=list(scratch.values()),
        compiler_params=pltpu.CompilerParams(collective_id=0, has_side_effects=True, vmem_limit_bytes=limit),
        cost_estimate=pl.CostEstimate(flops=4 * 10**9, bytes_accessed=10**7, transcendentals=0),
    )(*inputs.values())
    return pl.pallas_call(
        place,
        out_shape=outs,
        in_specs=[pl.BlockSpec(memory_space=pltpu.VMEM)] * 7,
        out_specs=[pl.BlockSpec(memory_space=pltpu.VMEM)] * 4,
    )(*results)


def solution(mesh):
    nc, nz = mesh.shape["cohort"], mesh.shape["snp"]
    in_specs = (
        P(None, "cohort"),
        P(None, "snp"),
        P("cohort"),
        P("cohort"),
        P("cohort"),
        P(),
        P("cohort"),
        P("cohort", "snp"),
        P(None, None, "cohort"),
        P(None, None, "snp"),
        P(),
        P(),
        P(),
        P(),
    )
    out_specs = (P(None, "cohort"), P(None, "snp"), P(None, "cohort"), P(None, "snp"))
    return jax.shard_map(
        functools.partial(body, nc, nz), mesh=mesh, in_specs=in_specs, out_specs=out_specs, check_vma=False
    )
```
